32 devices in a mesh: table: 16 (over z, y, x), seq: 2 (over core).
Axes of the slice: x: 2, y: 2, z: 4, core: 2. Of those that a mesh axis runs over, the one named last changes fastest.
Arguments:
- embed_table: bfloat16 [131072, 512], P('table')
- lookup_ids: int32 [16, 2, 16, 192], P('table', 'seq'), may hold values from 0 to 8191
- counts: int32 [16, 2, 16], P('table', 'seq'), may hold values from 0 to 192, as said below
- event_order: int32 [16, 2, 2048], P('table', 'seq'), may hold values from 0 to 2047, each once within a row
- hist_len: int32 [16], P('table'), may hold values from 1024 to 4096, as said below
- w_uvqk: bfloat16 [512, 2048], replicated, may hold values from -0.25 to 0.25
- w_out: bfloat16 [512, 512], replicated, may hold values from -0.25 to 0.25
Outputs:
- layer_out: bfloat16 [16, 4096, 512], P('table', 'seq')
The draws below stay inside these ranges and needn't reach their ends.
Inputs may be any that keep to these rules, and one draw needn't show every extreme that they name: For every user and piece the 16 counts sum to 2048; for every piece index one shard gets exactly 192 from every user. Only the first counts[u, p, j] slots of lookup_ids[u, p, j] are read. `hist_len`: some user has exactly 4096 events.
All inputs are finite; a program needn't handle non-finite values.
Results may differ from the reference program's by a relative error of at most 0.0039.
Values may be sent and summed in bfloat16 or wider, within the bound.
A program may use at most 128 MiB of HBM per device.

```python
import math
import jax
import jax.numpy as jnp
from jax import lax

D = 512
HEADS = 4
WINDOW = 1024
TOK_DEV = 2048
ROWS_SHARD = 8192
HEAD_DIM = 128
USERS = 16
PIECES = 2
SHARDS = 16
LENGTH = 4096
CAP = 192
ROWS = 131072


def draw_counts(key, part):
    remaining = TOK_DEV - CAP
    base_count = remaining // (SHARDS - 1)
    extra_count = remaining - base_count * (SHARDS - 1)
    key_hot, key_jitter = jax.random.split(jax.random.fold_in(key, 11))
    jitter = jax.random.randint(key_jitter, (USERS, PIECES, SHARDS - 1), 0, base_count // 2 + 1)
    others = base_count + jitter - jnp.roll(jitter, 1, axis=2)
    others = others + (jnp.arange(SHARDS - 1) < extra_count).astype(jnp.int32)[None, None, :]
    hot_shard = jax.random.randint(key_hot, (PIECES,), 0, SHARDS)
    column = jnp.arange(SHARDS)
    source_column = column[None, :] - (column[None, :] > hot_shard[:, None]).astype(jnp.int32)
    source_column = jnp.clip(source_column, 0, SHARDS - 2)
    source_column = jnp.broadcast_to(source_column[None], (USERS, PIECES, SHARDS))
    placed = jnp.take_along_axis(others, source_column, axis=2)
    return jnp.where(column[None, None, :] == hot_shard[None, :, None], CAP, placed).astype(jnp.int32)


def draw_hist_len(key, part):
    key_lengths, key_longest = jax.random.split(jax.random.fold_in(key, 23))
    lengths = jax.random.randint(key_lengths, (USERS,), LENGTH // 4, LENGTH + 1)
    longest = jax.random.randint(key_longest, (), 0, USERS)
    return jnp.where(jnp.arange(USERS) == longest, LENGTH, lengths).astype(jnp.int32)


def draw_embed_table(key, part):
    key_base, key_rows, key_columns = jax.random.split(jax.random.fold_in(key, 37), 3)
    row_scale = jnp.exp(jax.random.uniform(key_rows, (ROWS, 1), minval=math.log(0.3), maxval=math.log(3.0)))
    column_scale = jnp.exp(jax.random.uniform(key_columns, (1, D), minval=math.log(0.3), maxval=math.log(3.0)))
    base_values = jax.random.normal(key_base, (ROWS, D))
    return (base_values * row_scale * column_scale).astype(jnp.float32).astype(jnp.bfloat16)


def plant(entries, stream_key, smallest, high):
    dims = entries.shape
    spot = [jax.random.randint(jax.random.fold_in(stream_key, axis), (), 0, dims[axis]) for axis in range(len(dims))]
    entries = entries.at[tuple(spot)].set(smallest)
    longest = dims.index(max(dims))
    spot[longest] = (spot[longest] + 1) % dims[longest]
    return entries.at[tuple(spot)].set(high)


def normal_values(stream_key, dims, width, most, kind=jnp.bfloat16):
    entries = width * jax.random.normal(stream_key, dims, jnp.float32)
    return jnp.clip(entries, min=-most, max=most).astype(kind)


def setup_inputs(seed: int = 0) -> dict:
    streams_of = jax.random.split(jax.random.key(seed), 8)
    return {
        "embed_table": draw_embed_table(jax.random.fold_in(streams_of[7], 71), 0),
        "lookup_ids": plant(jax.random.randint(streams_of[1], (USERS, PIECES, SHARDS, CAP), 0, ROWS_SHARD), jax.random.fold_in(streams_of[1], 1), 0, ROWS_SHARD - 1).astype(jnp.int32),
        "counts": draw_counts(jax.random.fold_in(streams_of[7], 71), 0),
        "event_order": jax.vmap(lambda own: jax.random.permutation(own, TOK_DEV))(jax.random.split(streams_of[3], USERS * PIECES)).reshape((USERS, PIECES, TOK_DEV)).astype(jnp.int32),
        "hist_len": draw_hist_len(jax.random.fold_in(streams_of[7], 71), 0),
        "w_uvqk": normal_values(streams_of[5], (D, 4 * D), D ** -0.5, 0.25),
        "w_out": normal_values(streams_of[6], (D, D), D ** -0.5, 0.25),
    }


def normalize(values):
    average = lax.optimization_barrier(jnp.mean(values, axis=-1, keepdims=True))
    centered = values - average
    spread = lax.optimization_barrier(jnp.mean(centered * centered, axis=-1, keepdims=True))
    return centered * lax.rsqrt(spread + 1e-05)

def attend_block(queries, keyvals):
    query_rows = queries.shape[0]
    key_rows = keyvals.shape[0]
    query_heads = queries.reshape(query_rows, HEADS, HEAD_DIM).astype(jnp.float32)
    key_heads = keyvals[:, :D].reshape(key_rows, HEADS, HEAD_DIM).astype(jnp.float32)
    value_heads = keyvals[:, D:].reshape(key_rows, HEADS, HEAD_DIM).astype(jnp.float32)
    scores = jnp.einsum('qhd,khd->hqk', query_heads, key_heads) * HEAD_DIM ** (-0.5)
    distance = jnp.arange(query_rows)[:, None] + (key_rows - query_rows) - jnp.arange(key_rows)[None, :]
    inside = (distance >= 0) & (distance < key_rows - query_rows)
    weights = jnp.where(inside[None], jax.nn.silu(scores), 0.0).astype(jnp.bfloat16)
    attended = jnp.einsum('hqk,khd->qhd', weights.astype(jnp.float32), value_heads)
    return attended.reshape(query_rows, D)

def gather_events(embed_table, lookup_ids, counts, event_order):
    totals = jnp.cumsum(counts, axis=2)
    starts = totals - counts
    owner_shard = lax.optimization_barrier(jnp.sum((event_order[..., None] >= totals[:, :, None, :]).astype(jnp.int32), axis=3))
    slot_start = jnp.take_along_axis(starts, owner_shard, axis=2)
    slot_index = (owner_shard * CAP + event_order - slot_start).astype(jnp.int32)
    flat_ids = lookup_ids.reshape(USERS, PIECES, SHARDS * CAP)
    local_ids = jnp.take_along_axis(flat_ids, slot_index, axis=2)
    table_rows = (owner_shard * ROWS_SHARD + local_ids).astype(jnp.int32)
    return embed_table[table_rows.reshape(USERS, LENGTH)]

def user_layer(embedded, length, w_uvqk, w_out):
    normed = normalize(embedded.astype(jnp.float32)).astype(jnp.bfloat16)
    activated = jax.nn.silu(jnp.dot(normed, w_uvqk, preferred_element_type=jnp.float32)).astype(jnp.bfloat16)
    gate_part = activated[:, :D]
    queries = activated[:, D:2 * D]
    keyvals = activated[:, 2 * D:]
    padded = jnp.concatenate([jnp.zeros((WINDOW, 2 * D), jnp.bfloat16), keyvals], axis=0)

    def one_block(block_index):
        first = (block_index * WINDOW).astype(jnp.int32)
        query_block = lax.dynamic_slice_in_dim(queries, first, WINDOW, 0)
        key_block = lax.dynamic_slice_in_dim(padded, first, 2 * WINDOW, 0)
        return attend_block(query_block, key_block)
    attended = lax.map(one_block, jnp.arange(LENGTH // WINDOW, dtype=jnp.int32)).reshape(LENGTH, D)
    gated_rows = (normalize(attended) * gate_part.astype(jnp.float32)).astype(jnp.bfloat16)
    result = jnp.dot(gated_rows, w_out, preferred_element_type=jnp.float32) + embedded.astype(jnp.float32)
    inside = jnp.arange(LENGTH, dtype=jnp.int32) < length
    return jnp.where(inside[:, None], result, 0.0).astype(jnp.bfloat16)

def reference(embed_table, lookup_ids, counts, event_order, hist_len, w_uvqk, w_out):
    events = gather_events(embed_table, lookup_ids, counts, event_order)

    def per_user(user_pair):
        return user_layer(user_pair[0], user_pair[1], w_uvqk, w_out)
    return lax.map(per_user, (events, hist_len))
```

```python
import functools

import jax
import jax.numpy as jnp
from jax import lax
from jax.experimental import pallas as pl
from jax.experimental.pallas import tpu as pltpu
from jax.sharding import PartitionSpec as P

HEADS = 4
WINDOW = 1024
BLOCK = 256
VMEM_LIMIT = 48 * 1024 * 1024


def passed_along(value, axis, steps):
    count = lax.axis_size(axis)
    initial, last = (max(0, -steps), min(count, count - steps))
    return lax.ppermute(value, axis, [(source, source + steps) for source in range(initial, last)])


def normalize(values):
    average = jnp.mean(values, axis=-1, keepdims=True)
    centered = values - average
    spread = jnp.mean(centered * centered, axis=-1, keepdims=True)
    return centered * lax.rsqrt(spread + 1e-05)


def silu_of_double(half):
    return half + half * jnp.tanh(half)


def project_kernel(query_scale, events_ref, w_ref, gate_ref, query_ref, keyval_ref):
    width = events_ref.shape[1]
    normed = normalize(events_ref[...].astype(jnp.float32)).astype(jnp.bfloat16)

    def columns(first, count):
        product = jnp.dot(normed, w_ref[:, first : first + count], preferred_element_type=jnp.float32)
        return silu_of_double(0.5 * product)

    gate_ref[...] = columns(0, width).astype(gate_ref.dtype)
    query_ref[...] = (columns(width, width) * query_scale).astype(query_ref.dtype)
    keyval_ref[:, :width] = columns(2 * width, width).astype(keyval_ref.dtype)
    keyval_ref[:, width:] = columns(3 * width, width).astype(keyval_ref.dtype)


def project(events, w_uvqk):
    tokens, width = events.shape
    rows = 512
    query_scale = 0.5 * (width // HEADS) ** (-0.5)
    kind = jnp.bfloat16
    return pl.pallas_call(
        functools.partial(project_kernel, query_scale),
        grid=(tokens // rows,),
        in_specs=[
            pl.BlockSpec((rows, width), lambda i: (i, 0)),
            pl.BlockSpec((width, 4 * width), lambda i: (0, 0)),
        ],
        out_specs=[
            pl.BlockSpec((rows, width), lambda i: (i, 0)),
            pl.BlockSpec((rows, width), lambda i: (i, 0)),
            pl.BlockSpec((rows, 2 * width), lambda i: (i, 0)),
        ],
        out_shape=[
            jax.ShapeDtypeStruct((tokens, width), kind),
            jax.ShapeDtypeStruct((tokens, width), kind),
            jax.ShapeDtypeStruct((tokens, 2 * width), kind),
        ],
        compiler_params=pltpu.CompilerParams(vmem_limit_bytes=VMEM_LIMIT),
        cost_estimate=pl.CostEstimate(
            flops=8 * tokens * width * width,
            bytes_accessed=10 * tokens * width + 8 * width * width,
            transcendentals=4 * tokens * width,
        ),
        name="project",
    )(events, w_uvqk)


def scores_of(queries, keys):
    return lax.dot_general(
        queries, keys, (((1,), (1,)), ((), ())), preferred_element_type=jnp.float32
    )


def attend_kernel(live_ref, query_ref, before_ref, own_ref, gate_ref, events_ref, w_ref, *rest):
    out_ref, context, heads_out = rest[-3:]
    rows, width = query_ref.shape
    head_width = width // HEADS
    block = pl.program_id(0)

    @pl.when(block == 0)
    def _():
        context[:WINDOW] = before_ref[...]
        context[WINDOW:] = own_ref[...]

    row = lax.broadcasted_iota(jnp.int32, (rows, rows), 0)
    column = lax.broadcasted_iota(jnp.int32, (rows, rows), 1)
    near = column <= row
    near_weight = near.astype(jnp.float32).astype(jnp.bfloat16)
    first = pl.multiple_of(block * rows, rows)
    far_rows = pl.ds(first, rows)
    middle_rows = pl.ds(pl.multiple_of(first + rows, rows), WINDOW - rows)
    near_rows = pl.ds(pl.multiple_of(first + WINDOW, rows), rows)
    for head in range(HEADS):
        at = slice(head * head_width, (head + 1) * head_width)
        value_at = slice(width + head * head_width, width + (head + 1) * head_width)
        queries = query_ref[:, at]
        edge = jnp.where(
            near,
            scores_of(queries, context[near_rows, at]),
            scores_of(queries, context[far_rows, at]),
        )
        edge = silu_of_double(edge.astype(jnp.bfloat16))
        edge_near = edge * near_weight
        edge_far = edge - edge_near
        middle = scores_of(queries, context[middle_rows, at]).astype(jnp.bfloat16)
        middle = silu_of_double(middle)
        total = jnp.dot(middle, context[middle_rows, value_at], preferred_element_type=jnp.float32)
        total += jnp.dot(edge_near, context[near_rows, value_at], preferred_element_type=jnp.float32)
        total += jnp.dot(edge_far, context[far_rows, value_at], preferred_element_type=jnp.float32)
        heads_out[:, at] = total
    gated = normalize(heads_out[...]) * gate_ref[...].astype(jnp.float32)
    result = jnp.dot(gated.astype(jnp.bfloat16), w_ref[...], preferred_element_type=jnp.float32)
    result = result + events_ref[...].astype(jnp.float32)
    position = first + lax.broadcasted_iota(jnp.int32, (rows, 1), 0)
    out_ref[...] = jnp.where(position < live_ref[0], result, 0.0).astype(out_ref.dtype)


def attend(part, live, queries, before, keyvals, gate, events, w_out, partial_out):
    tokens, width = events.shape
    per_part = WINDOW // BLOCK
    rowed = pl.BlockSpec((BLOCK, width), lambda i: (part * per_part + i, 0))
    if before is None:
        before = keyvals
        before_spec = pl.BlockSpec((WINDOW, 2 * width), lambda i: (part - 1, 0))
    else:
        before_spec = pl.BlockSpec((WINDOW, 2 * width), lambda i: (0, 0))
    operands = [live, queries, before, keyvals, gate, events, w_out]
    in_specs = [
        pl.BlockSpec(memory_space=pltpu.SMEM),
        rowed,
        before_spec,
        pl.BlockSpec((WINDOW, 2 * width), lambda i: (part, 0)),
        rowed,
        rowed,
        pl.BlockSpec((width, width), lambda i: (0, 0)),
    ]
    aliases = {}
    if partial_out is not None:
        aliases = {len(operands): 0}
        operands.append(partial_out)
        in_specs.append(pl.BlockSpec(memory_space=pl.ANY))
    return pl.pallas_call(
        attend_kernel,
        grid=(per_part,),
        in_specs=in_specs,
        out_specs=rowed,
        out_shape=jax.ShapeDtypeStruct((tokens, width), jnp.bfloat16),
        scratch_shapes=[
            pltpu.VMEM((2 * WINDOW, 2 * width), jnp.bfloat16),
            pltpu.VMEM((BLOCK, width), jnp.float32),
        ],
        input_output_aliases=aliases,
        compiler_params=pltpu.CompilerParams(vmem_limit_bytes=VMEM_LIMIT),
        cost_estimate=pl.CostEstimate(
            flops=4 * WINDOW * (WINDOW + BLOCK) * width + 2 * WINDOW * width * width,
            bytes_accessed=16 * WINDOW * width + 2 * width * width,
            transcendentals=WINDOW * WINDOW * HEADS,
        ),
        name="attend",
    )(*operands)


def look_up(embed_table, lookup_ids, counts, event_order):
    shards = lax.axis_size("table")
    capacity = lookup_ids.shape[3]
    width = embed_table.shape[1]
    requests = lookup_ids[0, 0]
    fetched = lax.all_to_all(
        embed_table[lax.all_to_all(requests, "table", split_axis=0, concat_axis=0, tiled=True)],
        "table",
        split_axis=0,
        concat_axis=0,
        tiled=True,
    )
    live_counts = counts[0, 0]
    totals = jnp.cumsum(live_counts)
    starts = totals - live_counts
    event_rank = event_order[0, 0]
    owner_shard = jnp.sum((event_rank[:, None] >= totals[None, :]).astype(jnp.int32), axis=1)
    chosen = owner_shard[:, None] == jnp.arange(shards, dtype=jnp.int32)[None, :]
    slot_start = jnp.sum(jnp.where(chosen, starts[None, :], 0), axis=1)
    slot_index = owner_shard * capacity + event_rank - slot_start
    return fetched.reshape(shards * capacity, width)[slot_index]


def local(embed_table, lookup_ids, counts, event_order, hist_len, w_uvqk, w_out):
    events = look_up(embed_table, lookup_ids, counts, event_order)
    tokens = events.shape[0]
    gate, queries, keyvals = project(events, w_uvqk)
    before = passed_along(keyvals[tokens - WINDOW :], "seq", 1)
    live = hist_len - lax.axis_index("seq") * tokens
    out = None
    for part in reversed(range(tokens // WINDOW)):
        out = attend(
            part,
            live - part * WINDOW,
            queries,
            before if part == 0 else None,
            keyvals,
            gate,
            events,
            w_out,
            out,
        )
    return out[None]


def solution(mesh):
    in_specs = (
        P("table", None),
        P("table", "seq", None, None),
        P("table", "seq", None),
        P("table", "seq", None),
        P("table"),
        P(),
        P(),
    )
    out_specs = P("table", "seq", None)
    return jax.shard_map(local, mesh=mesh, in_specs=in_specs, out_specs=out_specs, check_vma=False)
```

```python
import functools

import jax
import jax.numpy as jnp
from jax import lax
from jax.experimental import pallas as pl
from jax.experimental.pallas import tpu as pltpu
from jax.sharding import PartitionSpec as P

HEADS = 4
WINDOW = 1024
BLOCK = 256
VMEM_LIMIT = 48 * 1024 * 1024
LOOK_UP_LIMIT = 56 * 1024 * 1024


def passed_along(value, axis, steps):
    count = lax.axis_size(axis)
    initial, last = (max(0, -steps), min(count, count - steps))
    return lax.ppermute(value, axis, [(source, source + steps) for source in range(initial, last)])


def normalize(values):
    average = jnp.mean(values, axis=-1, keepdims=True)
    centered = values - average
    spread = jnp.mean(centered * centered, axis=-1, keepdims=True)
    return centered * lax.rsqrt(spread + 1e-05)


def silu_of_double(half):
    return half + half * jnp.tanh(half)


def project_kernel(query_scale, events_ref, w_ref, gate_ref, query_ref, keyval_ref):
    width = events_ref.shape[1]
    normed = normalize(events_ref[...].astype(jnp.float32)).astype(jnp.bfloat16)

    def columns(first, count):
        product = jnp.dot(normed, w_ref[:, first : first + count], preferred_element_type=jnp.float32)
        return silu_of_double(0.5 * product)

    gate_ref[...] = columns(0, width).astype(gate_ref.dtype)
    query_ref[...] = (columns(width, width) * query_scale).astype(query_ref.dtype)
    keyval_ref[:, :width] = columns(2 * width, width).astype(keyval_ref.dtype)
    keyval_ref[:, width:] = columns(3 * width, width).astype(keyval_ref.dtype)


def project(events, w_uvqk):
    tokens, width = events.shape
    rows = 512
    query_scale = 0.5 * (width // HEADS) ** (-0.5)
    kind = jnp.bfloat16
    return pl.pallas_call(
        functools.partial(project_kernel, query_scale),
        grid=(tokens // rows,),
        in_specs=[
            pl.BlockSpec((rows, width), lambda i: (i, 0)),
            pl.BlockSpec((width, 4 * width), lambda i: (0, 0)),
        ],
        out_specs=[
            pl.BlockSpec((rows, width), lambda i: (i, 0)),
            pl.BlockSpec((rows, width), lambda i: (i, 0)),
            pl.BlockSpec((rows, 2 * width), lambda i: (i, 0)),
        ],
        out_shape=[
            jax.ShapeDtypeStruct((tokens, width), kind),
            jax.ShapeDtypeStruct((tokens, width), kind),
            jax.ShapeDtypeStruct((tokens, 2 * width), kind),
        ],
        compiler_params=pltpu.CompilerParams(vmem_limit_bytes=VMEM_LIMIT),
        cost_estimate=pl.CostEstimate(
            flops=8 * tokens * width * width,
            bytes_accessed=10 * tokens * width + 8 * width * width,
            transcendentals=4 * tokens * width,
        ),
        name="project",
    )(events, w_uvqk)


def scores_of(queries, keys):
    return lax.dot_general(
        queries, keys, (((1,), (1,)), ((), ())), preferred_element_type=jnp.float32
    )


def attend_kernel(live_ref, query_ref, before_ref, own_ref, gate_ref, events_ref, w_ref, *rest):
    out_ref, context, heads_out = rest[-3:]
    rows, width = query_ref.shape
    head_width = width // HEADS
    block = pl.program_id(0)

    @pl.when(block == 0)
    def _():
        context[:WINDOW] = before_ref[...]
        context[WINDOW:] = own_ref[...]

    row = lax.broadcasted_iota(jnp.int32, (rows, rows), 0)
    column = lax.broadcasted_iota(jnp.int32, (rows, rows), 1)
    near = column <= row
    near_weight = near.astype(jnp.float32).astype(jnp.bfloat16)
    first = pl.multiple_of(block * rows, rows)
    far_rows = pl.ds(first, rows)
    middle_rows = pl.ds(pl.multiple_of(first + rows, rows), WINDOW - rows)
    near_rows = pl.ds(pl.multiple_of(first + WINDOW, rows), rows)
    for head in range(HEADS):
        at = slice(head * head_width, (head + 1) * head_width)
        value_at = slice(width + head * head_width, width + (head + 1) * head_width)
        queries = query_ref[:, at]
        edge = jnp.where(
            near,
            scores_of(queries, context[near_rows, at]),
            scores_of(queries, context[far_rows, at]),
        )
        edge = silu_of_double(edge.astype(jnp.bfloat16))
        edge_near = edge * near_weight
        edge_far = edge - edge_near
        middle = scores_of(queries, context[middle_rows, at]).astype(jnp.bfloat16)
        middle = silu_of_double(middle)
        total = jnp.dot(middle, context[middle_rows, value_at], preferred_element_type=jnp.float32)
        total += jnp.dot(edge_near, context[near_rows, value_at], preferred_element_type=jnp.float32)
        total += jnp.dot(edge_far, context[far_rows, value_at], preferred_element_type=jnp.float32)
        heads_out[:, at] = total
    gated = normalize(heads_out[...]) * gate_ref[...].astype(jnp.float32)
    result = jnp.dot(gated.astype(jnp.bfloat16), w_ref[...], preferred_element_type=jnp.float32)
    result = result + events_ref[...].astype(jnp.float32)
    position = first + lax.broadcasted_iota(jnp.int32, (rows, 1), 0)
    out_ref[...] = jnp.where(position < live_ref[0], result, 0.0).astype(out_ref.dtype)


def attend(part, live, queries, before, keyvals, gate, events, w_out, partial_out):
    tokens, width = events.shape
    per_part = WINDOW // BLOCK
    rowed = pl.BlockSpec((BLOCK, width), lambda i: (part * per_part + i, 0))
    if before is None:
        before = keyvals
        before_spec = pl.BlockSpec((WINDOW, 2 * width), lambda i: (part - 1, 0))
    else:
        before_spec = pl.BlockSpec((WINDOW, 2 * width), lambda i: (0, 0))
    operands = [live, queries, before, keyvals, gate, events, w_out]
    in_specs = [
        pl.BlockSpec(memory_space=pltpu.SMEM),
        rowed,
        before_spec,
        pl.BlockSpec((WINDOW, 2 * width), lambda i: (part, 0)),
        rowed,
        rowed,
        pl.BlockSpec((width, width), lambda i: (0, 0)),
    ]
    aliases = {}
    if partial_out is not None:
        aliases = {len(operands): 0}
        operands.append(partial_out)
        in_specs.append(pl.BlockSpec(memory_space=pl.ANY))
    return pl.pallas_call(
        attend_kernel,
        grid=(per_part,),
        in_specs=in_specs,
        out_specs=rowed,
        out_shape=jax.ShapeDtypeStruct((tokens, width), jnp.bfloat16),
        scratch_shapes=[
            pltpu.VMEM((2 * WINDOW, 2 * width), jnp.bfloat16),
            pltpu.VMEM((BLOCK, width), jnp.float32),
        ],
        input_output_aliases=aliases,
        compiler_params=pltpu.CompilerParams(vmem_limit_bytes=VMEM_LIMIT),
        cost_estimate=pl.CostEstimate(
            flops=4 * WINDOW * (WINDOW + BLOCK) * width + 2 * WINDOW * width * width,
            bytes_accessed=16 * WINDOW * width + 2 * width * width,
            transcendentals=WINDOW * WINDOW * HEADS,
        ),
        name="attend",
    )(*operands)


def peer_offset(step, count):
    if count % 2:
        return step + 1
    away = (step + 1) // 2
    return count // 2 + away * (1 - 2 * (step % 2))


def look_up_kernel(
    ids_ref,
    keys_ref,
    rank_ref,
    table_ref,
    out_ref,
    ids_held,
    ids_scalar,
    staged,
    table_wide,
    rank_wide,
    rows_wide,
    sent,
    received,
    stage_sems,
    scalar_sem,
    ids_send_sems,
    ids_recv_sems,
    send_sems,
    recv_sems,
):
    shards, capacity, width = sent.shape
    tokens = out_ref.shape[0]
    parts, part_rows = staged.shape[0], staged.shape[1]
    me = lax.axis_index("table")
    mesh_ids = pl.DeviceIdType.MESH

    def stage(part):
        return pltpu.make_async_copy(
            table_ref.at[pl.ds(pl.multiple_of(part * part_rows, part_rows), part_rows)],
            staged.at[part],
            stage_sems.at[part],
        )

    for part in range(parts):
        stage(part).start()

    barrier = pltpu.get_barrier_semaphore()

    @pl.loop(1, shards)
    def _(offset):
        peer = lax.rem(me + offset, shards)
        pl.semaphore_signal(barrier, inc=1, device_id={"table": peer}, device_id_type=mesh_ids)

    pl.semaphore_wait(barrier, shards - 1)

    def send_ids(offset):
        peer = lax.rem(me + offset, shards)
        return pltpu.make_async_remote_copy(
            src_ref=ids_ref.at[peer],
            dst_ref=ids_held.at[me],
            send_sem=ids_send_sems.at[offset],
            recv_sem=ids_recv_sems.at[me],
            device_id={"table": peer},
            device_id_type=mesh_ids,
        )

    def take_ids(source):
        return pltpu.make_async_remote_copy(
            src_ref=ids_ref.at[source],
            dst_ref=ids_held.at[source],
            send_sem=ids_send_sems.at[0],
            recv_sem=ids_recv_sems.at[source],
            device_id={"table": source},
            device_id_type=mesh_ids,
        )

    @pl.loop(1, shards)
    def _(offset):
        send_ids(offset).start()

    ids_held[me] = ids_ref[me]
    rank_wide[...] = jnp.broadcast_to(rank_ref[...], rank_wide.shape)

    for part in range(parts):
        stage(part).wait()

        @pl.loop(0, part_rows, step=64)
        def _(first):
            first = pl.multiple_of(first, 64)
            target = pl.multiple_of(part * part_rows + first, 64)
            table_wide[pl.ds(target, 64)] = staged[part, pl.ds(first, 64)].astype(jnp.float32)

    @pl.loop(1, shards)
    def _(offset):
        take_ids(lax.rem(me + offset, shards)).wait_recv()

    to_scalar = pltpu.make_async_copy(ids_held, ids_scalar, scalar_sem)
    to_scalar.start()
    to_scalar.wait()

    def gather(peer):
        @pl.loop(0, capacity, step=16)
        def _(first):
            for i in range(16):
                row = ids_scalar[peer, 0, first + i]
                rows_wide[pl.ds(first + i, 1)] = table_wide[pl.ds(row, 1)]

        return rows_wide[...].astype(jnp.bfloat16)

    def send_rows(offset):
        peer = lax.rem(me + offset, shards)
        return pltpu.make_async_remote_copy(
            src_ref=sent.at[offset],
            dst_ref=received.at[me],
            send_sem=send_sems.at[offset],
            recv_sem=recv_sems.at[me],
            device_id={"table": peer},
            device_id_type=mesh_ids,
        )

    def take_rows(source):
        return pltpu.make_async_remote_copy(
            src_ref=sent.at[0],
            dst_ref=received.at[source],
            send_sem=send_sems.at[0],
            recv_sem=recv_sems.at[source],
            device_id={"table": source},
            device_id_type=mesh_ids,
        )

    @pl.loop(0, shards - 1)
    def _(step):
        offset = peer_offset(step, shards)
        sent[offset] = gather(lax.rem(me + offset, shards))
        send_rows(offset).start()

    received[me] = gather(me)

    def place(source, add):
        keys = keys_ref[source]

        @pl.loop(0, tokens, step=256)
        def _(first):
            at = pl.ds(pl.multiple_of(first, 256), 256)
            chosen = jnp.where(rank_wide[at] == keys, 1.0, 0.0).astype(jnp.bfloat16)
            found = jnp.dot(chosen, received[source], preferred_element_type=jnp.float32)
            found = found.astype(jnp.bfloat16)
            out_ref[at] = out_ref[at] + found if add else found

    place(me, False)

    @pl.loop(0, shards - 1)
    def _(step):
        source = lax.rem(me + shards - peer_offset(step, shards), shards)
        take_rows(source).wait_recv()
        place(source, True)

    @pl.loop(1, shards)
    def _(offset):
        send_ids(offset).wait_send()
        send_rows(offset).wait_send()


def look_up(embed_table, lookup_ids, counts, event_order):
    shards = lax.axis_size("table")
    capacity = lookup_ids.shape[3]
    tokens = event_order.shape[2]
    rows, width = embed_table.shape
    parts = 8 if rows % 1024 == 0 else 1
    live_counts = counts[0, 0]
    starts = jnp.cumsum(live_counts) - live_counts
    slots = jnp.arange(capacity, dtype=jnp.int32)
    keys = jnp.where(slots < live_counts[:, None], starts[:, None] + slots, -1)
    vmem = pl.BlockSpec(memory_space=pltpu.VMEM)
    return pl.pallas_call(
        look_up_kernel,
        in_specs=[vmem, vmem, vmem, pl.BlockSpec(memory_space=pl.ANY)],
        out_specs=vmem,
        out_shape=jax.ShapeDtypeStruct((tokens, width), jnp.bfloat16),
        scratch_shapes=[
            pltpu.VMEM((shards, 1, capacity), jnp.int32),
            pltpu.SMEM((shards, 1, capacity), jnp.int32),
            pltpu.VMEM((parts, rows // parts, width), jnp.bfloat16),
            pltpu.VMEM((rows, width), jnp.float32),
            pltpu.VMEM((tokens, capacity), jnp.int32),
            pltpu.VMEM((capacity, width), jnp.float32),
            pltpu.VMEM((shards, capacity, width), jnp.bfloat16),
            pltpu.VMEM((shards, capacity, width), jnp.bfloat16),
            pltpu.SemaphoreType.DMA((parts,)),
            pltpu.SemaphoreType.DMA,
            pltpu.SemaphoreType.DMA((shards,)),
            pltpu.SemaphoreType.DMA((shards,)),
            pltpu.SemaphoreType.DMA((shards,)),
            pltpu.SemaphoreType.DMA((shards,)),
        ],
        compiler_params=pltpu.CompilerParams(
            collective_id=0, has_side_effects=True, vmem_limit_bytes=LOOK_UP_LIMIT
        ),
        cost_estimate=pl.CostEstimate(
            flops=2 * tokens * shards * capacity * width,
            bytes_accessed=2 * rows * width + 4 * shards * capacity * width,
            transcendentals=0,
        ),
        name="look_up",
    )(lookup_ids[0, 0][:, None, :], keys[:, None, :], event_order[0, 0][:, None], embed_table)


def local(embed_table, lookup_ids, counts, event_order, hist_len, w_uvqk, w_out):
    events = look_up(embed_table, lookup_ids, counts, event_order)
    tokens = events.shape[0]
    gate, queries, keyvals = project(events, w_uvqk)
    before = passed_along(keyvals[tokens - WINDOW :], "seq", 1)
    live = hist_len - lax.axis_index("seq") * tokens
    out = None
    for part in reversed(range(tokens // WINDOW)):
        out = attend(
            part,
            live - part * WINDOW,
            queries,
            before if part == 0 else None,
            keyvals,
            gate,
            events,
            w_out,
            out,
        )
    return out[None]


def solution(mesh):
    in_specs = (
        P("table", None),
        P("table", "seq", None, None),
        P("table", "seq", None),
        P("table", "seq", None),
        P("table"),
        P(),
        P(),
    )
    out_specs = P("table", "seq", None)
    return jax.shard_map(local, mesh=mesh, in_specs=in_specs, out_specs=out_specs, check_vma=False)
```

```python
import functools

import jax
import jax.numpy as jnp
from jax import lax
from jax.experimental import pallas as pl
from jax.experimental.pallas import tpu as pltpu
from jax.sharding import PartitionSpec as P

HEADS = 4
WINDOW = 1024
BLOCK = 256
LANES = 128
VMEM_LIMIT = 48 * 1024 * 1024
LOOK_UP_LIMIT = 56 * 1024 * 1024


def passed_along(value, axis, steps):
    count = lax.axis_size(axis)
    initial, last = (max(0, -steps), min(count, count - steps))
    return lax.ppermute(value, axis, [(source, source + steps) for source in range(initial, last)])


def normalize(values):
    average = jnp.mean(values, axis=-1, keepdims=True)
    centered = values - average
    spread = jnp.mean(centered * centered, axis=-1, keepdims=True)
    return centered * lax.rsqrt(spread + 1e-05)


def silu_of_double(half):
    return half + half * jnp.tanh(half)


def project_kernel(query_scale, events_ref, w_ref, gate_ref, query_ref, keyval_ref, last_ref):
    width = events_ref.shape[1]
    normed = normalize(events_ref[...].astype(jnp.float32)).astype(jnp.bfloat16)

    def columns(first, count):
        product = jnp.dot(normed, w_ref[:, first : first + count], preferred_element_type=jnp.float32)
        return silu_of_double(0.5 * product)

    gate_ref[...] = columns(0, width).astype(gate_ref.dtype)
    query_ref[...] = (columns(width, width) * query_scale).astype(query_ref.dtype)
    keyval_ref[:, :width] = columns(2 * width, width).astype(keyval_ref.dtype)
    keyval_ref[:, width:] = columns(3 * width, width).astype(keyval_ref.dtype)

    @pl.when(pl.program_id(0) >= pl.num_programs(0) - WINDOW // events_ref.shape[0])
    def _():
        last_ref[...] = keyval_ref[...]


def project(events, w_uvqk):
    tokens, width = events.shape
    rows = 512
    skipped = (tokens - WINDOW) // rows
    query_scale = 0.5 * (width // HEADS) ** (-0.5)
    kind = jnp.bfloat16
    return pl.pallas_call(
        functools.partial(project_kernel, query_scale),
        grid=(tokens // rows,),
        in_specs=[
            pl.BlockSpec((rows, width), lambda i: (i, 0)),
            pl.BlockSpec((width, 4 * width), lambda i: (0, 0)),
        ],
        out_specs=[
            pl.BlockSpec((rows, width), lambda i: (i, 0)),
            pl.BlockSpec((rows, width), lambda i: (i, 0)),
            pl.BlockSpec((rows, 2 * width), lambda i: (i, 0)),
            pl.BlockSpec((rows, 2 * width), lambda i: (jnp.maximum(i - skipped, 0), 0)),
        ],
        out_shape=[
            jax.ShapeDtypeStruct((tokens, width), kind),
            jax.ShapeDtypeStruct((tokens, width), kind),
            jax.ShapeDtypeStruct((tokens, 2 * width), kind),
            jax.ShapeDtypeStruct((WINDOW, 2 * width), kind),
        ],
        compiler_params=pltpu.CompilerParams(vmem_limit_bytes=VMEM_LIMIT),
        cost_estimate=pl.CostEstimate(
            flops=8 * tokens * width * width,
            bytes_accessed=10 * tokens * width + 8 * width * width,
            transcendentals=4 * tokens * width,
        ),
        name="project",
    )(events, w_uvqk)


def scores_of(queries, keys):
    return lax.dot_general(
        queries, keys, (((1,), (1,)), ((), ())), preferred_element_type=jnp.float32
    )


def attend_kernel(live_ref, query_ref, before_ref, own_ref, gate_ref, events_ref, w_ref, *rest):
    out_ref, context, heads_out = rest[-3:]
    rows, width = query_ref.shape
    head_width = width // HEADS
    block = pl.program_id(0)

    @pl.when(block == 0)
    def _():
        context[:WINDOW] = before_ref[...]
        context[WINDOW:] = own_ref[...]

    row = lax.broadcasted_iota(jnp.int32, (rows, rows), 0)
    column = lax.broadcasted_iota(jnp.int32, (rows, rows), 1)
    near = column <= row
    near_weight = near.astype(jnp.float32).astype(jnp.bfloat16)
    first = pl.multiple_of(block * rows, rows)
    far_rows = pl.ds(first, rows)
    middle_rows = pl.ds(pl.multiple_of(first + rows, rows), WINDOW - rows)
    near_rows = pl.ds(pl.multiple_of(first + WINDOW, rows), rows)
    for head in range(HEADS):
        at = slice(head * head_width, (head + 1) * head_width)
        value_at = slice(width + head * head_width, width + (head + 1) * head_width)
        queries = query_ref[:, at]
        edge = jnp.where(
            near,
            scores_of(queries, context[near_rows, at]),
            scores_of(queries, context[far_rows, at]),
        )
        edge = silu_of_double(edge.astype(jnp.bfloat16))
        edge_near = edge * near_weight
        edge_far = edge - edge_near
        middle = scores_of(queries, context[middle_rows, at]).astype(jnp.bfloat16)
        middle = silu_of_double(middle)
        total = jnp.dot(middle, context[middle_rows, value_at], preferred_element_type=jnp.float32)
        total += jnp.dot(edge_near, context[near_rows, value_at], preferred_element_type=jnp.float32)
        total += jnp.dot(edge_far, context[far_rows, value_at], preferred_element_type=jnp.float32)
        heads_out[:, at] = total
    gated = normalize(heads_out[...]) * gate_ref[...].astype(jnp.float32)
    result = jnp.dot(gated.astype(jnp.bfloat16), w_ref[...], preferred_element_type=jnp.float32)
    result = result + events_ref[...].astype(jnp.float32)
    position = first + lax.broadcasted_iota(jnp.int32, (rows, 1), 0)
    out_ref[...] = jnp.where(position < live_ref[0], result, 0.0).astype(out_ref.dtype)


def attend(part, live, queries, before, keyvals, gate, events, w_out, partial_out):
    tokens, width = events.shape
    per_part = WINDOW // BLOCK
    rowed = pl.BlockSpec((BLOCK, width), lambda i: (part * per_part + i, 0))
    if before is None:
        before = keyvals
        before_spec = pl.BlockSpec((WINDOW, 2 * width), lambda i: (part - 1, 0))
    else:
        before_spec = pl.BlockSpec((WINDOW, 2 * width), lambda i: (0, 0))
    operands = [live, queries, before, keyvals, gate, events, w_out]
    in_specs = [
        pl.BlockSpec(memory_space=pltpu.SMEM),
        rowed,
        before_spec,
        pl.BlockSpec((WINDOW, 2 * width), lambda i: (part, 0)),
        rowed,
        rowed,
        pl.BlockSpec((width, width), lambda i: (0, 0)),
    ]
    aliases = {}
    if partial_out is not None:
        aliases = {len(operands): 0}
        operands.append(partial_out)
        in_specs.append(pl.BlockSpec(memory_space=pl.ANY))
    return pl.pallas_call(
        attend_kernel,
        grid=(per_part,),
        in_specs=in_specs,
        out_specs=rowed,
        out_shape=jax.ShapeDtypeStruct((tokens, width), jnp.bfloat16),
        scratch_shapes=[
            pltpu.VMEM((2 * WINDOW, 2 * width), jnp.bfloat16),
            pltpu.VMEM((BLOCK, width), jnp.float32),
        ],
        input_output_aliases=aliases,
        compiler_params=pltpu.CompilerParams(vmem_limit_bytes=VMEM_LIMIT),
        cost_estimate=pl.CostEstimate(
            flops=4 * WINDOW * (WINDOW + BLOCK) * width + 2 * WINDOW * width * width,
            bytes_accessed=16 * WINDOW * width + 2 * width * width,
            transcendentals=WINDOW * WINDOW * HEADS,
        ),
        name="attend",
    )(*operands)


def peer_offset(step, count):
    if count % 2:
        return step + 1
    turn = step // 2
    away = (turn + 1) // 2
    far = count // 2 + away * (1 - 2 * (turn % 2))
    near = lax.rem(count - 1 - turn // 2 + (turn % 2) * (turn + 1), count)
    return jnp.where(step % 2 == 0, far, near)


def look_up_kernel(
    lookup_ref,
    counts_ref,
    order_ref,
    table_ref,
    out_ref,
    ids_ref,
    starts,
    ids_held,
    ids_scalar,
    staged,
    table_wide,
    rank_wide,
    rows_wide,
    sent,
    received,
    stage_sems,
    scalar_sem,
    ids_send_sems,
    ids_recv_sems,
    send_sems,
    recv_sems,
):
    shards, capacity, width = sent.shape
    tokens = out_ref.shape[0]
    parts, part_rows = staged.shape[0], staged.shape[1]
    me = lax.axis_index("table")
    mesh_ids = pl.DeviceIdType.MESH

    def stage(part):
        return pltpu.make_async_copy(
            table_ref.at[pl.ds(pl.multiple_of(part * part_rows, part_rows), part_rows)],
            staged.at[part],
            stage_sems.at[part],
        )

    for part in range(parts):
        stage(part).start()

    for shard in range(shards):
        ids_ref[shard] = lookup_ref[0, 0, shard : shard + 1]

    barrier = pltpu.get_barrier_semaphore()

    @pl.loop(1, shards)
    def _(offset):
        peer = lax.rem(me + offset, shards)
        pl.semaphore_signal(barrier, inc=1, device_id={"table": peer}, device_id_type=mesh_ids)

    pl.semaphore_wait(barrier, shards - 1)

    def send_ids(offset):
        peer = lax.rem(me + offset, shards)
        return pltpu.make_async_remote_copy(
            src_ref=ids_ref.at[peer],
            dst_ref=ids_held.at[me],
            send_sem=ids_send_sems.at[offset],
            recv_sem=ids_recv_sems.at[me],
            device_id={"table": peer},
            device_id_type=mesh_ids,
        )

    def take_ids(source):
        return pltpu.make_async_remote_copy(
            src_ref=ids_ref.at[source],
            dst_ref=ids_held.at[source],
            send_sem=ids_send_sems.at[0],
            recv_sem=ids_recv_sems.at[source],
            device_id={"table": source},
            device_id_type=mesh_ids,
        )

    @pl.loop(1, shards)
    def _(offset):
        send_ids(offset).start()

    ids_held[me] = ids_ref[me]
    start = jnp.int32(0)
    for shard in range(shards):
        starts[shard] = start
        start = start + counts_ref[0, 0, shard]

    for first in range(0, tokens, LANES):
        ranks = order_ref[0, :, first : first + LANES]
        ranks = jnp.transpose(jnp.broadcast_to(ranks, (LANES, LANES)))
        for column in range(0, capacity, LANES):
            count = min(LANES, capacity - column)
            rank_wide[first : first + LANES, column : column + count] = ranks[:, :count]

    for part in range(parts):
        stage(part).wait()

        @pl.loop(0, part_rows, step=64)
        def _(first):
            first = pl.multiple_of(first, 64)
            target = pl.multiple_of(part * part_rows + first, 64)
            table_wide[pl.ds(target, 64)] = staged[part, pl.ds(first, 64)].astype(jnp.float32)

    @pl.loop(1, shards)
    def _(offset):
        take_ids(lax.rem(me + offset, shards)).wait_recv()

    to_scalar = pltpu.make_async_copy(ids_held, ids_scalar, scalar_sem)
    to_scalar.start()
    to_scalar.wait()

    def gather(peer):
        @pl.loop(0, capacity, step=16)
        def _(first):
            for i in range(16):
                row = ids_scalar[peer, 0, first + i]
                rows_wide[pl.ds(first + i, 1)] = table_wide[pl.ds(row, 1)]

        return rows_wide[...].astype(jnp.bfloat16)

    def send_rows(offset):
        peer = lax.rem(me + offset, shards)
        return pltpu.make_async_remote_copy(
            src_ref=sent.at[offset],
            dst_ref=received.at[me],
            send_sem=send_sems.at[offset],
            recv_sem=recv_sems.at[me],
            device_id={"table": peer},
            device_id_type=mesh_ids,
        )

    def take_rows(source):
        return pltpu.make_async_remote_copy(
            src_ref=sent.at[0],
            dst_ref=received.at[source],
            send_sem=send_sems.at[0],
            recv_sem=recv_sems.at[source],
            device_id={"table": source},
            device_id_type=mesh_ids,
        )

    @pl.loop(0, shards - 1)
    def _(step):
        offset = peer_offset(step, shards)
        sent[offset] = gather(lax.rem(me + offset, shards))
        send_rows(offset).start()

    received[me] = gather(me)

    def place(source, add):
        slot = lax.broadcasted_iota(jnp.int32, (1, capacity), 1)
        keys = jnp.where(slot < counts_ref[0, 0, source], starts[source] + slot, -1)

        @pl.loop(0, tokens, step=256)
        def _(first):
            at = pl.ds(pl.multiple_of(first, 256), 256)
            chosen = jnp.where(rank_wide[at] == keys, 1.0, 0.0).astype(jnp.bfloat16)
            found = jnp.dot(chosen, received[source], preferred_element_type=jnp.float32)
            found = found.astype(jnp.bfloat16)
            out_ref[at] = out_ref[at] + found if add else found

    place(me, False)

    @pl.loop(0, shards - 1)
    def _(step):
        source = lax.rem(me + shards - peer_offset(step, shards), shards)
        take_rows(source).wait_recv()
        place(source, True)

    @pl.loop(1, shards)
    def _(offset):
        send_ids(offset).wait_send()
        send_rows(offset).wait_send()


def look_up(embed_table, lookup_ids, counts, event_order):
    shards = lax.axis_size("table")
    capacity = lookup_ids.shape[3]
    tokens = event_order.shape[2]
    rows, width = embed_table.shape
    parts = 8 if rows % 1024 == 0 else 1
    vmem = pl.BlockSpec(memory_space=pltpu.VMEM)
    return pl.pallas_call(
        look_up_kernel,
        in_specs=[
            vmem,
            pl.BlockSpec(memory_space=pltpu.SMEM),
            vmem,
            pl.BlockSpec(memory_space=pl.ANY),
        ],
        out_specs=vmem,
        out_shape=jax.ShapeDtypeStruct((tokens, width), jnp.bfloat16),
        scratch_shapes=[
            pltpu.VMEM((shards, 1, capacity), jnp.int32),
            pltpu.SMEM((shards,), jnp.int32),
            pltpu.VMEM((shards, 1, capacity), jnp.int32),
            pltpu.SMEM((shards, 1, capacity), jnp.int32),
            pltpu.VMEM((parts, rows // parts, width), jnp.bfloat16),
            pltpu.VMEM((rows, width), jnp.float32),
            pltpu.VMEM((tokens, capacity), jnp.int32),
            pltpu.VMEM((capacity, width), jnp.float32),
            pltpu.VMEM((shards, capacity, width), jnp.bfloat16),
            pltpu.VMEM((shards, capacity, width), jnp.bfloat16),
            pltpu.SemaphoreType.DMA((parts,)),
            pltpu.SemaphoreType.DMA,
            pltpu.SemaphoreType.DMA((shards,)),
            pltpu.SemaphoreType.DMA((shards,)),
            pltpu.SemaphoreType.DMA((shards,)),
            pltpu.SemaphoreType.DMA((shards,)),
        ],
        compiler_params=pltpu.CompilerParams(
            collective_id=0, has_side_effects=True, vmem_limit_bytes=LOOK_UP_LIMIT
        ),
        cost_estimate=pl.CostEstimate(
            flops=2 * tokens * shards * capacity * width,
            bytes_accessed=2 * rows * width + 4 * shards * capacity * width,
            transcendentals=0,
        ),
        name="look_up",
    )(lookup_ids, counts, event_order, embed_table)


def local(embed_table, lookup_ids, counts, event_order, hist_len, w_uvqk, w_out):
    events = look_up(embed_table, lookup_ids, counts, event_order)
    tokens = events.shape[0]
    gate, queries, keyvals, last = project(events, w_uvqk)
    before = passed_along(last, "seq", 1)
    live = hist_len - lax.axis_index("seq") * tokens
    out = None
    for part in reversed(range(tokens // WINDOW)):
        out = attend(
            part,
            live - part * WINDOW,
            queries,
            before if part == 0 else None,
            keyvals,
            gate,
            events,
            w_out,
            out,
        )
    return out[None]


def solution(mesh):
    in_specs = (
        P("table", None),
        P("table", "seq", None, None),
        P("table", "seq", None),
        P("table", "seq", None),
        P("table"),
        P(),
        P(),
    )
    out_specs = P("table", "seq", None)
    return jax.shard_map(local, mesh=mesh, in_specs=in_specs, out_specs=out_specs, check_vma=False)
```

```python
import jax
import jax.numpy as jnp
from jax import lax
from jax.experimental import pallas as pl
from jax.experimental.pallas import tpu as pltpu
from jax.sharding import PartitionSpec as P

HEADS = 4
WINDOW = 1024
BLOCK = 256
LANES = 128
VMEM_LIMIT = 60 * 1024 * 1024


def normalize(values):
    average = jnp.mean(values, axis=-1, keepdims=True)
    centered = values - average
    spread = jnp.mean(centered * centered, axis=-1, keepdims=True)
    return centered * lax.rsqrt(spread + 1e-05)


def silu_of_double(half):
    return half + half * jnp.tanh(half)


def scores_of(queries, keys):
    return lax.dot_general(
        queries, keys, (((1,), (1,)), ((), ())), preferred_element_type=jnp.float32
    )


def dot32(left, right):
    return jnp.dot(left, right, preferred_element_type=jnp.float32)


def peer_offset(step, count):
    if count % 2:
        return step + 1
    turn = step // 2
    away = (turn + 1) // 2
    far = count // 2 + away * (1 - 2 * (turn % 2))
    near = lax.rem(count - 1 - turn // 2 + (turn % 2) * (turn + 1), count)
    return jnp.where(step % 2 == 0, far, near)


def layer_kernel(
    lookup_ref,
    counts_ref,
    order_ref,
    live_ref,
    table_ref,
    w_in_ref,
    w_out_ref,
    out_ref,
    ids_ref,
    starts,
    ids_held,
    ids_scalar,
    staged,
    table_wide,
    rank_wide,
    rows_wide,
    sent,
    received,
    stage_sems,
    scalar_sem,
    ids_send_sems,
    ids_recv_sems,
    send_sems,
    recv_sems,
    w_in,
    w_out,
    weight_sems,
    events,
    gate,
    queries,
    context,
    heads_out,
    result,
    result_sems,
    halo_send_sem,
    halo_recv_sem,
):
    shards, capacity, width = sent.shape
    tokens = events.shape[0]
    slots, part_rows = staged.shape[0], staged.shape[1]
    parts = table_ref.shape[0] // part_rows
    me = lax.axis_index("table")
    piece, pieces = lax.axis_index("seq"), lax.axis_size("seq")
    mesh_ids = pl.DeviceIdType.MESH

    def stage(part):
        return pltpu.make_async_copy(
            table_ref.at[pl.ds(pl.multiple_of(part * part_rows, part_rows), part_rows)],
            staged.at[part % slots],
            stage_sems.at[part % slots],
        )

    for part in range(slots):
        stage(part).start()
    load_in = pltpu.make_async_copy(w_in_ref, w_in, weight_sems.at[0])
    load_out = pltpu.make_async_copy(w_out_ref, w_out, weight_sems.at[1])
    load_in.start()
    load_out.start()

    for shard in range(shards):
        ids_ref[shard] = lookup_ref[0, 0, shard : shard + 1]

    barrier = pltpu.get_barrier_semaphore()

    @pl.loop(1, shards)
    def _(offset):
        peer = lax.rem(me + offset, shards)
        pl.semaphore_signal(barrier, inc=1, device_id={"table": peer}, device_id_type=mesh_ids)

    @pl.when(piece > 0)
    def _():
        pl.semaphore_signal(barrier, inc=1, device_id={"seq": piece - 1}, device_id_type=mesh_ids)

    @pl.when(piece < pieces - 1)
    def _():
        pl.semaphore_signal(barrier, inc=1, device_id={"seq": piece + 1}, device_id_type=mesh_ids)

    neighbours = jnp.where(piece > 0, 1, 0) + jnp.where(piece < pieces - 1, 1, 0)
    pl.semaphore_wait(barrier, shards - 1 + neighbours)

    def send_ids(offset):
        peer = lax.rem(me + offset, shards)
        return pltpu.make_async_remote_copy(
            src_ref=ids_ref.at[peer],
            dst_ref=ids_held.at[me],
            send_sem=ids_send_sems.at[offset],
            recv_sem=ids_recv_sems.at[me],
            device_id={"table": peer},
            device_id_type=mesh_ids,
        )

    def take_ids(source):
        return pltpu.make_async_remote_copy(
            src_ref=ids_ref.at[source],
            dst_ref=ids_held.at[source],
            send_sem=ids_send_sems.at[0],
            recv_sem=ids_recv_sems.at[source],
            device_id={"table": source},
            device_id_type=mesh_ids,
        )

    @pl.loop(1, shards)
    def _(offset):
        send_ids(offset).start()

    ids_held[me] = ids_ref[me]
    start = jnp.int32(0)
    for shard in range(shards):
        starts[shard] = start
        start = start + counts_ref[0, 0, shard]

    for first in range(0, tokens, LANES):
        ranks = order_ref[0, :, first : first + LANES]
        ranks = jnp.transpose(jnp.broadcast_to(ranks, (LANES, LANES)))
        for column in range(0, capacity, LANES):
            count = min(LANES, capacity - column)
            rank_wide[first : first + LANES, column : column + count] = ranks[:, :count]

    for part in range(parts):
        stage(part).wait()

        @pl.loop(0, part_rows, step=64)
        def _(first):
            first = pl.multiple_of(first, 64)
            target = pl.multiple_of(part * part_rows + first, 64)
            table_wide[pl.ds(target, 64)] = staged[part % slots, pl.ds(first, 64)].astype(
                jnp.float32
            )

        if part + slots < parts:
            stage(part + slots).start()

    @pl.loop(1, shards)
    def _(offset):
        take_ids(lax.rem(me + offset, shards)).wait_recv()

    to_scalar = pltpu.make_async_copy(ids_held, ids_scalar, scalar_sem)
    to_scalar.start()
    to_scalar.wait()

    def gather(peer):
        @pl.loop(0, capacity, step=16)
        def _(first):
            for i in range(16):
                row = ids_scalar[peer, 0, first + i]
                rows_wide[pl.ds(first + i, 1)] = table_wide[pl.ds(row, 1)]

        return rows_wide[...].astype(jnp.bfloat16)

    def send_rows(offset):
        peer = lax.rem(me + offset, shards)
        return pltpu.make_async_remote_copy(
            src_ref=sent.at[offset],
            dst_ref=received.at[me],
            send_sem=send_sems.at[offset],
            recv_sem=recv_sems.at[me],
            device_id={"table": peer},
            device_id_type=mesh_ids,
        )

    def take_rows(source):
        return pltpu.make_async_remote_copy(
            src_ref=sent.at[0],
            dst_ref=received.at[source],
            send_sem=send_sems.at[0],
            recv_sem=recv_sems.at[source],
            device_id={"table": source},
            device_id_type=mesh_ids,
        )

    @pl.loop(0, shards - 1)
    def _(step):
        offset = peer_offset(step, shards)
        sent[offset] = gather(lax.rem(me + offset, shards))
        send_rows(offset).start()

    received[me] = gather(me)

    def place(source, add):
        slot = lax.broadcasted_iota(jnp.int32, (1, capacity), 1)
        keys = jnp.where(slot < counts_ref[0, 0, source], starts[source] + slot, -1)

        @pl.loop(0, tokens, step=256)
        def _(first):
            at = pl.ds(pl.multiple_of(first, 256), 256)
            chosen = jnp.where(rank_wide[at] == keys, 1.0, 0.0).astype(jnp.bfloat16)
            found = jnp.dot(chosen, received[source], preferred_element_type=jnp.float32)
            found = found.astype(jnp.bfloat16)
            events[at] = events[at] + found if add else found

    place(me, False)

    @pl.loop(0, shards - 1)
    def _(step):
        source = lax.rem(me + shards - peer_offset(step, shards), shards)
        take_rows(source).wait_recv()
        place(source, True)

    @pl.loop(1, shards)
    def _(offset):
        send_ids(offset).wait_send()
        send_rows(offset).wait_send()

    load_in.wait()
    load_out.wait()
    query_scale = 0.5 * (width // HEADS) ** (-0.5)
    blocks = tokens // BLOCK
    skipped = WINDOW // BLOCK

    def block_at(block, offset=0):
        return pl.ds(pl.multiple_of(block * BLOCK + offset, BLOCK), BLOCK)

    def project(block):
        at = block_at(block)
        normed = normalize(events[at].astype(jnp.float32)).astype(jnp.bfloat16)

        def columns(first):
            weights = w_in[:, first : first + width]
            product = jnp.dot(normed, weights, preferred_element_type=jnp.float32)
            return silu_of_double(0.5 * product)

        gate[at] = columns(0).astype(gate.dtype)
        queries[at] = (columns(width) * query_scale).astype(queries.dtype)
        own = block_at(block, WINDOW)
        context[own, :width] = columns(2 * width).astype(context.dtype)
        context[own, width:] = columns(3 * width).astype(context.dtype)

    @pl.loop(blocks - skipped, blocks)
    def _(block):
        project(block)

    halo = pltpu.make_async_remote_copy(
        src_ref=context.at[pl.ds(tokens, WINDOW)],
        dst_ref=context.at[pl.ds(0, WINDOW)],
        send_sem=halo_send_sem,
        recv_sem=halo_recv_sem,
        device_id={"seq": lax.rem(piece + 1, pieces)},
        device_id_type=mesh_ids,
    )

    @pl.when(piece < pieces - 1)
    def _():
        halo.start()

    @pl.loop(0, blocks - skipped)
    def _(block):
        project(block)

    row = lax.broadcasted_iota(jnp.int32, (BLOCK, BLOCK), 0)
    column = lax.broadcasted_iota(jnp.int32, (BLOCK, BLOCK), 1)
    near = column <= row
    near_weight = near.astype(jnp.float32).astype(jnp.bfloat16)
    head_width = width // HEADS

    def attend(block):
        at = block_at(block)
        far_rows = at
        middle_rows = pl.ds(pl.multiple_of((block + 1) * BLOCK, BLOCK), WINDOW - BLOCK)
        near_rows = block_at(block, WINDOW)
        for head in range(HEADS):
            of = slice(head * head_width, (head + 1) * head_width)
            value_of = slice(width + head * head_width, width + (head + 1) * head_width)
            asked = queries[at, of]
            edge = jnp.where(
                near,
                scores_of(asked, context[near_rows, of]),
                scores_of(asked, context[far_rows, of]),
            )
            edge = silu_of_double(edge.astype(jnp.bfloat16))
            edge_near = edge * near_weight
            edge_far = edge - edge_near
            middle = silu_of_double(scores_of(asked, context[middle_rows, of]).astype(jnp.bfloat16))
            total = dot32(middle, context[middle_rows, value_of])
            total += dot32(edge_near, context[near_rows, value_of])
            total += dot32(edge_far, context[far_rows, value_of])
            heads_out[:, of] = total
        gated = normalize(heads_out[...]) * gate[at].astype(jnp.float32)
        layer = dot32(gated.astype(jnp.bfloat16), w_out[...]) + events[at].astype(jnp.float32)
        position = piece * tokens + block * BLOCK + lax.broadcasted_iota(jnp.int32, (BLOCK, 1), 0)
        result[at] = jnp.where(position < live_ref[0], layer, 0.0).astype(result.dtype)

    def write(block):
        at = block_at(block)
        return pltpu.make_async_copy(result.at[at], out_ref.at[0, at], result_sems.at[block])

    @pl.loop(skipped, blocks)
    def _(block):
        attend(block)
        write(block).start()

    @pl.when(piece > 0)
    def _():
        halo.wait_recv()

    @pl.when(piece == 0)
    def _():
        context[:WINDOW] = jnp.zeros((WINDOW, 2 * width), context.dtype)

    @pl.loop(0, skipped)
    def _(block):
        attend(block)
        write(block).start()

    @pl.when(piece < pieces - 1)
    def _():
        halo.wait_send()

    @pl.loop(0, blocks)
    def _(block):
        write(block).wait()


def local(embed_table, lookup_ids, counts, event_order, hist_len, w_uvqk, w_out):
    shards = lax.axis_size("table")
    capacity = lookup_ids.shape[3]
    tokens = event_order.shape[2]
    rows, width = embed_table.shape
    part_rows = 1024 if rows % 1024 == 0 else rows
    slots = min(2, rows // part_rows)
    kind = jnp.bfloat16
    vmem = pl.BlockSpec(memory_space=pltpu.VMEM)
    smem = pl.BlockSpec(memory_space=pltpu.SMEM)
    anywhere = pl.BlockSpec(memory_space=pl.ANY)
    dma = pltpu.SemaphoreType.DMA
    return pl.pallas_call(
        layer_kernel,
        in_specs=[vmem, smem, vmem, smem, anywhere, anywhere, anywhere],
        out_specs=anywhere,
        out_shape=jax.ShapeDtypeStruct((1, tokens, width), kind),
        scratch_shapes=[
            pltpu.VMEM((shards, 1, capacity), jnp.int32),
            pltpu.SMEM((shards,), jnp.int32),
            pltpu.VMEM((shards, 1, capacity), jnp.int32),
            pltpu.SMEM((shards, 1, capacity), jnp.int32),
            pltpu.VMEM((slots, part_rows, width), kind),
            pltpu.VMEM((rows, width), jnp.float32),
            pltpu.VMEM((tokens, capacity), jnp.int32),
            pltpu.VMEM((capacity, width), jnp.float32),
            pltpu.VMEM((shards, capacity, width), kind),
            pltpu.VMEM((shards, capacity, width), kind),
            dma((slots,)),
            dma,
            dma((shards,)),
            dma((shards,)),
            dma((shards,)),
            dma((shards,)),
            pltpu.VMEM(w_uvqk.shape, kind),
            pltpu.VMEM(w_out.shape, kind),
            dma((2,)),
            pltpu.VMEM((tokens, width), kind),
            pltpu.VMEM((tokens, width), kind),
            pltpu.VMEM((tokens, width), kind),
            pltpu.VMEM((WINDOW + tokens, 2 * width), kind),
            pltpu.VMEM((BLOCK, width), jnp.float32),
            pltpu.VMEM((tokens, width), kind),
            dma((tokens // BLOCK,)),
            dma,
            dma,
        ],
        compiler_params=pltpu.CompilerParams(
            collective_id=0, has_side_effects=True, vmem_limit_bytes=VMEM_LIMIT
        ),
        cost_estimate=pl.CostEstimate(
            flops=2 * tokens * shards * capacity * width
            + 10 * tokens * width * width
            + 4 * tokens * (WINDOW + BLOCK) * width,
            bytes_accessed=2 * rows * width + 2 * tokens * width + 10 * width * width,
            transcendentals=4 * tokens * width + tokens * WINDOW * HEADS,
        ),
        name="layer",
    )(lookup_ids, counts, event_order, hist_len, embed_table, w_uvqk, w_out)


def solution(mesh):
    in_specs = (
        P("table", None),
        P("table", "seq", None, None),
        P("table", "seq", None),
        P("table", "seq", None),
        P("table"),
        P(),
        P(),
    )
    out_specs = P("table", "seq", None)
    return jax.shard_map(local, mesh=mesh, in_specs=in_specs, out_specs=out_specs, check_vma=False)
```

```python
import jax
import jax.numpy as jnp
from jax import lax
from jax.experimental import pallas as pl
from jax.experimental.pallas import tpu as pltpu
from jax.sharding import PartitionSpec as P

HEADS = 4
WINDOW = 1024
BLOCK = 256
PAIR = 2 * BLOCK
PLACED = 1024
LANES = 128
VMEM_LIMIT = 60 * 1024 * 1024


def normalize(values):
    average = jnp.mean(values, axis=-1, keepdims=True)
    centered = values - average
    spread = jnp.mean(centered * centered, axis=-1, keepdims=True)
    return centered * lax.rsqrt(spread + 1e-05)


def silu_of_double(half):
    return half + half * jnp.tanh(half)


def scores_of(queries, keys):
    return lax.dot_general(
        queries, keys, (((1,), (1,)), ((), ())), preferred_element_type=jnp.float32
    )


def dot32(left, right):
    return jnp.dot(left, right, preferred_element_type=jnp.float32)


def peer_offset(step, count):
    if count % 2:
        return step + 1
    turn = step // 2
    away = (turn + 1) // 2
    far = count // 2 + away * (1 - 2 * (turn % 2))
    near = lax.rem(count - 1 - turn // 2 + (turn % 2) * (turn + 1), count)
    return jnp.where(step % 2 == 0, far, near)


def layer_kernel(
    lookup_ref,
    counts_ref,
    order_ref,
    live_ref,
    table_ref,
    w_in_ref,
    w_out_ref,
    out_ref,
    ids_ref,
    starts,
    ids_held,
    ids_scalar,
    staged,
    table_wide,
    rank_wide,
    rows_wide,
    sent,
    received,
    stage_sems,
    scalar_sem,
    ids_send_sems,
    ids_recv_sems,
    send_sems,
    recv_sems,
    w_in,
    w_out,
    weight_sems,
    events,
    gate,
    queries,
    context,
    heads_out,
    result,
    result_sems,
    halo_send_sem,
    halo_recv_sem,
):
    shards, capacity, width = sent.shape
    tokens = events.shape[0]
    slots, part_rows = staged.shape[0], staged.shape[1]
    parts = table_ref.shape[0] // part_rows
    me = lax.axis_index("table")
    piece, pieces = lax.axis_index("seq"), lax.axis_size("seq")
    mesh_ids = pl.DeviceIdType.MESH

    def stage(part):
        return pltpu.make_async_copy(
            table_ref.at[pl.ds(pl.multiple_of(part * part_rows, part_rows), part_rows)],
            staged.at[part % slots],
            stage_sems.at[part % slots],
        )

    for part in range(slots):
        stage(part).start()
    load_in = pltpu.make_async_copy(w_in_ref, w_in, weight_sems.at[0])
    load_out = pltpu.make_async_copy(w_out_ref, w_out, weight_sems.at[1])
    load_in.start()
    load_out.start()

    for shard in range(shards):
        ids_ref[shard] = lookup_ref[0, 0, shard : shard + 1]

    barrier = pltpu.get_barrier_semaphore()

    @pl.loop(1, shards)
    def _(offset):
        peer = lax.rem(me + offset, shards)
        pl.semaphore_signal(barrier, inc=1, device_id={"table": peer}, device_id_type=mesh_ids)

    @pl.when(piece > 0)
    def _():
        pl.semaphore_signal(barrier, inc=1, device_id={"seq": piece - 1}, device_id_type=mesh_ids)

    @pl.when(piece < pieces - 1)
    def _():
        pl.semaphore_signal(barrier, inc=1, device_id={"seq": piece + 1}, device_id_type=mesh_ids)

    neighbours = jnp.where(piece > 0, 1, 0) + jnp.where(piece < pieces - 1, 1, 0)
    pl.semaphore_wait(barrier, shards - 1 + neighbours)

    def send_ids(offset):
        peer = lax.rem(me + offset, shards)
        return pltpu.make_async_remote_copy(
            src_ref=ids_ref.at[peer],
            dst_ref=ids_held.at[me],
            send_sem=ids_send_sems.at[offset],
            recv_sem=ids_recv_sems.at[me],
            device_id={"table": peer},
            device_id_type=mesh_ids,
        )

    def take_ids(source):
        return pltpu.make_async_remote_copy(
            src_ref=ids_ref.at[source],
            dst_ref=ids_held.at[source],
            send_sem=ids_send_sems.at[0],
            recv_sem=ids_recv_sems.at[source],
            device_id={"table": source},
            device_id_type=mesh_ids,
        )

    @pl.loop(1, shards)
    def _(offset):
        send_ids(offset).start()

    ids_held[me] = ids_ref[me]
    start = jnp.int32(0)
    for shard in range(shards):
        starts[shard] = start
        start = start + counts_ref[0, 0, shard]

    for first in range(0, tokens, LANES):
        ranks = order_ref[0, :, first : first + LANES]
        ranks = jnp.transpose(jnp.broadcast_to(ranks, (LANES, LANES)))
        for column in range(0, capacity, LANES):
            count = min(LANES, capacity - column)
            rank_wide[first : first + LANES, column : column + count] = ranks[:, :count]

    for part in range(parts):
        stage(part).wait()

        @pl.loop(0, part_rows, step=64)
        def _(first):
            first = pl.multiple_of(first, 64)
            target = pl.multiple_of(part * part_rows + first, 64)
            table_wide[pl.ds(target, 64)] = staged[part % slots, pl.ds(first, 64)].astype(
                jnp.float32
            )

        if part + slots < parts:
            stage(part + slots).start()

    @pl.loop(1, shards)
    def _(offset):
        take_ids(lax.rem(me + offset, shards)).wait_recv()

    to_scalar = pltpu.make_async_copy(ids_held, ids_scalar, scalar_sem)
    to_scalar.start()
    to_scalar.wait()

    def gather(peer):
        @pl.loop(0, capacity, step=16)
        def _(first):
            for i in range(16):
                row = ids_scalar[peer, 0, first + i]
                rows_wide[pl.ds(first + i, 1)] = table_wide[pl.ds(row, 1)]

        return rows_wide[...].astype(jnp.bfloat16)

    def send_rows(offset):
        peer = lax.rem(me + offset, shards)
        return pltpu.make_async_remote_copy(
            src_ref=sent.at[offset],
            dst_ref=received.at[me],
            send_sem=send_sems.at[offset],
            recv_sem=recv_sems.at[me],
            device_id={"table": peer},
            device_id_type=mesh_ids,
        )

    def take_rows(source):
        return pltpu.make_async_remote_copy(
            src_ref=sent.at[0],
            dst_ref=received.at[source],
            send_sem=send_sems.at[0],
            recv_sem=recv_sems.at[source],
            device_id={"table": source},
            device_id_type=mesh_ids,
        )

    @pl.loop(0, shards - 1)
    def _(step):
        offset = peer_offset(step, shards)
        sent[offset] = gather(lax.rem(me + offset, shards))
        send_rows(offset).start()

    received[me] = gather(me)

    def place(source, add):
        slot = lax.broadcasted_iota(jnp.int32, (1, capacity), 1)
        keys = jnp.where(slot < counts_ref[0, 0, source], starts[source] + slot, -1)

        @pl.loop(0, tokens, step=PLACED)
        def _(first):
            at = pl.ds(pl.multiple_of(first, PLACED), PLACED)
            chosen = jnp.where(rank_wide[at] == keys, 1.0, 0.0).astype(jnp.bfloat16)
            found = jnp.dot(chosen, received[source], preferred_element_type=jnp.float32)
            found = found.astype(jnp.bfloat16)
            events[at] = events[at] + found if add else found

    place(me, False)

    @pl.loop(0, shards - 1)
    def _(step):
        source = lax.rem(me + shards - peer_offset(step, shards), shards)
        take_rows(source).wait_recv()
        place(source, True)

    @pl.loop(1, shards)
    def _(offset):
        send_ids(offset).wait_send()
        send_rows(offset).wait_send()

    load_in.wait()
    load_out.wait()
    query_scale = 0.5 * (width // HEADS) ** (-0.5)
    blocks = tokens // PAIR
    skipped = WINDOW // PAIR

    def block_at(block, offset=0, count=PAIR):
        return pl.ds(pl.multiple_of(block * PAIR + offset, BLOCK), count)

    def project(block):
        at = block_at(block)
        normed = (0.5 * normalize(events[at].astype(jnp.float32))).astype(jnp.bfloat16)

        def columns(first):
            return silu_of_double(dot32(normed, w_in[:, first : first + width]))

        gate[at] = columns(0).astype(gate.dtype)
        queries[at] = (columns(width) * query_scale).astype(queries.dtype)
        own = block_at(block, WINDOW)
        context[own, :width] = columns(2 * width).astype(context.dtype)
        context[own, width:] = columns(3 * width).astype(context.dtype)

    @pl.loop(blocks - skipped, blocks)
    def _(block):
        project(block)

    halo = pltpu.make_async_remote_copy(
        src_ref=context.at[pl.ds(tokens, WINDOW)],
        dst_ref=context.at[pl.ds(0, WINDOW)],
        send_sem=halo_send_sem,
        recv_sem=halo_recv_sem,
        device_id={"seq": lax.rem(piece + 1, pieces)},
        device_id_type=mesh_ids,
    )

    @pl.when(piece < pieces - 1)
    def _():
        halo.start()

    @pl.loop(0, blocks - skipped)
    def _(block):
        project(block)

    row = lax.broadcasted_iota(jnp.int32, (BLOCK, BLOCK), 0)
    column = lax.broadcasted_iota(jnp.int32, (BLOCK, BLOCK), 1)
    near = column <= row
    near_weight = near.astype(jnp.float32).astype(jnp.bfloat16)
    head_width = width // HEADS

    def attend(block):
        at = block_at(block)
        oldest = block_at(block, 0, BLOCK)
        newest = block_at(block, WINDOW + BLOCK, BLOCK)
        shared = block_at(block, BLOCK, WINDOW)
        for head in range(HEADS):
            of = slice(head * head_width, (head + 1) * head_width)
            value_of = slice(width + head * head_width, width + (head + 1) * head_width)
            asked = queries[at, of]
            whole = scores_of(asked, context[shared, of])
            upper_far = scores_of(asked[:BLOCK], context[oldest, of])
            lower_near = scores_of(asked[BLOCK:], context[newest, of])
            upper_edge = jnp.where(near, whole[:BLOCK, WINDOW - BLOCK :], upper_far)
            lower_edge = jnp.where(near, lower_near, whole[BLOCK:, :BLOCK])
            upper_edge = silu_of_double(upper_edge.astype(jnp.bfloat16))
            lower_edge = silu_of_double(lower_edge.astype(jnp.bfloat16))
            upper_near = upper_edge * near_weight
            lower_near = lower_edge * near_weight
            upper = silu_of_double(whole[:BLOCK, : WINDOW - BLOCK].astype(jnp.bfloat16))
            lower = silu_of_double(whole[BLOCK:, BLOCK:].astype(jnp.bfloat16))
            weights = jnp.concatenate(
                [
                    jnp.concatenate([upper, upper_near], axis=1),
                    jnp.concatenate([lower_edge - lower_near, lower], axis=1),
                ],
                axis=0,
            )
            total = dot32(weights, context[shared, value_of])
            heads_out[:BLOCK, of] = total[:BLOCK] + dot32(
                upper_edge - upper_near, context[oldest, value_of]
            )
            heads_out[BLOCK:, of] = total[BLOCK:] + dot32(lower_near, context[newest, value_of])
        gated = normalize(heads_out[...]) * gate[at].astype(jnp.float32)
        layer = dot32(gated.astype(jnp.bfloat16), w_out[...]) + events[at].astype(jnp.float32)
        position = piece * tokens + block * PAIR + lax.broadcasted_iota(jnp.int32, (PAIR, 1), 0)
        result[at] = jnp.where(position < live_ref[0], layer, 0.0).astype(result.dtype)

    def write(block):
        at = block_at(block)
        return pltpu.make_async_copy(result.at[at], out_ref.at[0, at], result_sems.at[block])

    @pl.loop(skipped, blocks)
    def _(block):
        attend(block)
        write(block).start()

    @pl.when(piece > 0)
    def _():
        halo.wait_recv()

    @pl.when(piece == 0)
    def _():
        context[:WINDOW] = jnp.zeros((WINDOW, 2 * width), context.dtype)

    @pl.loop(0, skipped)
    def _(block):
        attend(block)
        write(block).start()

    @pl.when(piece < pieces - 1)
    def _():
        halo.wait_send()

    @pl.loop(0, blocks)
    def _(block):
        write(block).wait()


def local(embed_table, lookup_ids, counts, event_order, hist_len, w_uvqk, w_out):
    shards = lax.axis_size("table")
    capacity = lookup_ids.shape[3]
    tokens = event_order.shape[2]
    rows, width = embed_table.shape
    part_rows = 1024 if rows % 1024 == 0 else rows
    slots = min(4, rows // part_rows)
    kind = jnp.bfloat16
    vmem = pl.BlockSpec(memory_space=pltpu.VMEM)
    smem = pl.BlockSpec(memory_space=pltpu.SMEM)
    anywhere = pl.BlockSpec(memory_space=pl.ANY)
    dma = pltpu.SemaphoreType.DMA
    return pl.pallas_call(
        layer_kernel,
        in_specs=[vmem, smem, vmem, smem, anywhere, anywhere, anywhere],
        out_specs=anywhere,
        out_shape=jax.ShapeDtypeStruct((1, tokens, width), kind),
        scratch_shapes=[
            pltpu.VMEM((shards, 1, capacity), jnp.int32),
            pltpu.SMEM((shards,), jnp.int32),
            pltpu.VMEM((shards, 1, capacity), jnp.int32),
            pltpu.SMEM((shards, 1, capacity), jnp.int32),
            pltpu.VMEM((slots, part_rows, width), kind),
            pltpu.VMEM((rows, width), jnp.float32),
            pltpu.VMEM((tokens, capacity), jnp.int32),
            pltpu.VMEM((capacity, width), jnp.float32),
            pltpu.VMEM((shards, capacity, width), kind),
            pltpu.VMEM((shards, capacity, width), kind),
            dma((slots,)),
            dma,
            dma((shards,)),
            dma((shards,)),
            dma((shards,)),
            dma((shards,)),
            pltpu.VMEM(w_uvqk.shape, kind),
            pltpu.VMEM(w_out.shape, kind),
            dma((2,)),
            pltpu.VMEM((tokens, width), kind),
            pltpu.VMEM((tokens, width), kind),
            pltpu.VMEM((tokens, width), kind),
            pltpu.VMEM((WINDOW + tokens, 2 * width), kind),
            pltpu.VMEM((PAIR, width), jnp.float32),
            pltpu.VMEM((tokens, width), kind),
            dma((tokens // PAIR,)),
            dma,
            dma,
        ],
        compiler_params=pltpu.CompilerParams(
            collective_id=0, has_side_effects=True, vmem_limit_bytes=VMEM_LIMIT
        ),
        cost_estimate=pl.CostEstimate(
            flops=2 * tokens * shards * capacity * width
            + 10 * tokens * width * width
            + 4 * tokens * (WINDOW + BLOCK) * width,
            bytes_accessed=2 * rows * width + 2 * tokens * width + 10 * width * width,
            transcendentals=4 * tokens * width + tokens * WINDOW * HEADS,
        ),
        name="layer",
    )(lookup_ids, counts, event_order, hist_len, embed_table, w_uvqk, w_out)


def solution(mesh):
    in_specs = (
        P("table", None),
        P("table", "seq", None, None),
        P("table", "seq", None),
        P("table", "seq", None),
        P("table"),
        P(),
        P(),
    )
    out_specs = P("table", "seq", None)
    return jax.shard_map(local, mesh=mesh, in_specs=in_specs, out_specs=out_specs, check_vma=False)
```

```python
import jax
import jax.numpy as jnp
from jax import lax
from jax.experimental import pallas as pl
from jax.experimental.pallas import tpu as pltpu
from jax.sharding import PartitionSpec as P

HEADS = 4
WINDOW = 1024
BLOCK = 256
PAIR = 2 * BLOCK
PLACED = 2048
LANES = 128
VMEM_LIMIT = 60 * 1024 * 1024


def normalize(values):
    average = jnp.mean(values, axis=-1, keepdims=True)
    centered = values - average
    spread = jnp.mean(centered * centered, axis=-1, keepdims=True)
    return centered * lax.rsqrt(spread + 1e-05)


def silu_of_double(half):
    return half + half * jnp.tanh(half)


def scores_of(queries, keys):
    return lax.dot_general(
        queries, keys, (((1,), (1,)), ((), ())), preferred_element_type=jnp.float32
    )


def dot32(left, right):
    return jnp.dot(left, right, preferred_element_type=jnp.float32)


def peer_offset(step, count):
    if count % 2:
        return step + 1
    turn = step // 2
    away = (turn + 1) // 2
    far = count // 2 + away * (1 - 2 * (turn % 2))
    near = lax.rem(count - 1 - turn // 2 + (turn % 2) * (turn + 1), count)
    return jnp.where(step % 2 == 0, far, near)


def layer_kernel(
    lookup_ref,
    counts_ref,
    order_ref,
    live_ref,
    table_ref,
    w_in_ref,
    w_out_ref,
    out_ref,
    ids_ref,
    starts,
    ids_held,
    ids_scalar,
    staged,
    table_wide,
    rank_wide,
    rows_wide,
    sent,
    received,
    stage_sems,
    scalar_sem,
    ids_send_sems,
    ids_recv_sems,
    send_sems,
    recv_sems,
    w_in,
    w_out,
    weight_sems,
    events,
    gate,
    queries,
    context,
    heads_out,
    result,
    result_sems,
    halo_send_sem,
    halo_recv_sem,
):
    shards, capacity, width = sent.shape
    tokens = events.shape[0]
    slots, part_rows = staged.shape[0], staged.shape[1]
    parts = table_ref.shape[0] // part_rows
    me = lax.axis_index("table")
    piece, pieces = lax.axis_index("seq"), lax.axis_size("seq")
    mesh_ids = pl.DeviceIdType.MESH

    def stage(part):
        return pltpu.make_async_copy(
            table_ref.at[pl.ds(pl.multiple_of(part * part_rows, part_rows), part_rows)],
            staged.at[part % slots],
            stage_sems.at[part % slots],
        )

    for part in range(slots):
        stage(part).start()
    load_in = pltpu.make_async_copy(w_in_ref, w_in, weight_sems.at[0])
    load_out = pltpu.make_async_copy(w_out_ref, w_out, weight_sems.at[1])
    load_in.start()
    load_out.start()

    for shard in range(shards):
        ids_ref[shard] = lookup_ref[0, 0, shard : shard + 1]

    barrier = pltpu.get_barrier_semaphore()

    @pl.loop(1, shards)
    def _(offset):
        peer = lax.rem(me + offset, shards)
        pl.semaphore_signal(barrier, inc=1, device_id={"table": peer}, device_id_type=mesh_ids)

    @pl.when(piece > 0)
    def _():
        pl.semaphore_signal(barrier, inc=1, device_id={"seq": piece - 1}, device_id_type=mesh_ids)

    @pl.when(piece < pieces - 1)
    def _():
        pl.semaphore_signal(barrier, inc=1, device_id={"seq": piece + 1}, device_id_type=mesh_ids)

    neighbours = jnp.where(piece > 0, 1, 0) + jnp.where(piece < pieces - 1, 1, 0)
    pl.semaphore_wait(barrier, shards - 1 + neighbours)

    def send_ids(offset):
        peer = lax.rem(me + offset, shards)
        return pltpu.make_async_remote_copy(
            src_ref=ids_ref.at[peer],
            dst_ref=ids_held.at[me],
            send_sem=ids_send_sems.at[offset],
            recv_sem=ids_recv_sems.at[me],
            device_id={"table": peer},
            device_id_type=mesh_ids,
        )

    def take_ids(source):
        return pltpu.make_async_remote_copy(
            src_ref=ids_ref.at[source],
            dst_ref=ids_held.at[source],
            send_sem=ids_send_sems.at[0],
            recv_sem=ids_recv_sems.at[source],
            device_id={"table": source},
            device_id_type=mesh_ids,
        )

    @pl.loop(1, shards)
    def _(offset):
        send_ids(offset).start()

    ids_held[me] = ids_ref[me]
    start = jnp.int32(0)
    for shard in range(shards):
        starts[shard] = start
        start = start + counts_ref[0, 0, shard]

    for first in range(0, tokens, LANES):
        ranks = order_ref[0, :, first : first + LANES]
        ranks = jnp.transpose(jnp.broadcast_to(ranks, (LANES, LANES)))
        for column in range(0, capacity, LANES):
            count = min(LANES, capacity - column)
            rank_wide[first : first + LANES, column : column + count] = ranks[:, :count]

    for part in range(parts):
        stage(part).wait()

        @pl.loop(0, part_rows, step=64)
        def _(first):
            first = pl.multiple_of(first, 64)
            target = pl.multiple_of(part * part_rows + first, 64)
            table_wide[pl.ds(target, 64)] = staged[part % slots, pl.ds(first, 64)].astype(
                jnp.float32
            )

        if part + slots < parts:
            stage(part + slots).start()

    @pl.loop(1, shards)
    def _(offset):
        take_ids(lax.rem(me + offset, shards)).wait_recv()

    to_scalar = pltpu.make_async_copy(ids_held, ids_scalar, scalar_sem)
    to_scalar.start()
    to_scalar.wait()

    def gather(peer):
        @pl.loop(0, capacity, step=16)
        def _(first):
            for i in range(16):
                row = ids_scalar[peer, 0, first + i]
                rows_wide[pl.ds(first + i, 1)] = table_wide[pl.ds(row, 1)]

        return rows_wide[...].astype(jnp.bfloat16)

    def send_rows(offset):
        peer = lax.rem(me + offset, shards)
        return pltpu.make_async_remote_copy(
            src_ref=sent.at[offset],
            dst_ref=received.at[me],
            send_sem=send_sems.at[offset],
            recv_sem=recv_sems.at[me],
            device_id={"table": peer},
            device_id_type=mesh_ids,
        )

    def take_rows(source):
        return pltpu.make_async_remote_copy(
            src_ref=sent.at[0],
            dst_ref=received.at[source],
            send_sem=send_sems.at[0],
            recv_sem=recv_sems.at[source],
            device_id={"table": source},
            device_id_type=mesh_ids,
        )

    @pl.loop(0, shards - 1)
    def _(step):
        offset = peer_offset(step, shards)
        sent[offset] = gather(lax.rem(me + offset, shards))
        send_rows(offset).start()

    received[me] = gather(me)

    def place(source, add):
        slot = lax.broadcasted_iota(jnp.int32, (1, capacity), 1)
        keys = jnp.where(slot < counts_ref[0, 0, source], starts[source] + slot, -1)

        for first in range(0, tokens, PLACED):
            at = slice(first, first + PLACED)
            chosen = jnp.where(rank_wide[at] == keys, 1.0, 0.0).astype(jnp.bfloat16)
            found = jnp.dot(chosen, received[source], preferred_element_type=jnp.float32)
            found = found.astype(jnp.bfloat16)
            events[at] = events[at] + found if add else found

    place(me, False)

    @pl.loop(0, shards - 1)
    def _(step):
        source = lax.rem(me + shards - peer_offset(step, shards), shards)
        take_rows(source).wait_recv()
        place(source, True)

    @pl.loop(1, shards)
    def _(offset):
        send_ids(offset).wait_send()
        send_rows(offset).wait_send()

    load_in.wait()
    load_out.wait()
    query_scale = 0.5 * (width // HEADS) ** (-0.5)
    blocks = tokens // PAIR
    skipped = WINDOW // PAIR

    def block_at(block, offset=0, count=PAIR):
        first = block * PAIR + offset
        return pl.ds(first if isinstance(first, int) else pl.multiple_of(first, BLOCK), count)

    def project(block):
        at = block_at(block)
        normed = (0.5 * normalize(events[at].astype(jnp.float32))).astype(jnp.bfloat16)

        def columns(first, kind):
            return silu_of_double(dot32(normed, w_in[:, first : first + width]).astype(kind))

        gate[at] = columns(0, jnp.float32).astype(gate.dtype)
        queries[at] = (columns(width, jnp.bfloat16).astype(jnp.float32) * query_scale).astype(queries.dtype)
        own = block_at(block, WINDOW)
        context[own, :width] = columns(2 * width, context.dtype)
        context[own, width:] = columns(3 * width, context.dtype)

    for block in range(blocks - skipped, blocks):
        project(block)

    halo = pltpu.make_async_remote_copy(
        src_ref=context.at[pl.ds(tokens, WINDOW)],
        dst_ref=context.at[pl.ds(0, WINDOW)],
        send_sem=halo_send_sem,
        recv_sem=halo_recv_sem,
        device_id={"seq": lax.rem(piece + 1, pieces)},
        device_id_type=mesh_ids,
    )

    @pl.when(piece < pieces - 1)
    def _():
        halo.start()

    for block in range(blocks - skipped):
        project(block)

    row = lax.broadcasted_iota(jnp.int32, (BLOCK, BLOCK), 0)
    column = lax.broadcasted_iota(jnp.int32, (BLOCK, BLOCK), 1)
    near = column <= row
    near_weight = near.astype(jnp.float32).astype(jnp.bfloat16)
    head_width = width // HEADS

    def attend(block):
        at = block_at(block)
        oldest = block_at(block, 0, BLOCK)
        newest = block_at(block, WINDOW + BLOCK, BLOCK)
        shared = block_at(block, BLOCK, WINDOW)
        for head in range(HEADS):
            of = slice(head * head_width, (head + 1) * head_width)
            value_of = slice(width + head * head_width, width + (head + 1) * head_width)
            asked = queries[at, of]
            whole = scores_of(asked, context[shared, of])
            upper_far = scores_of(asked[:BLOCK], context[oldest, of])
            lower_near = scores_of(asked[BLOCK:], context[newest, of])
            upper_edge = jnp.where(near, whole[:BLOCK, WINDOW - BLOCK :], upper_far)
            lower_edge = jnp.where(near, lower_near, whole[BLOCK:, :BLOCK])
            upper_edge = silu_of_double(upper_edge.astype(jnp.bfloat16))
            lower_edge = silu_of_double(lower_edge.astype(jnp.bfloat16))
            upper_near = upper_edge * near_weight
            lower_near = lower_edge * near_weight
            upper = silu_of_double(whole[:BLOCK, : WINDOW - BLOCK].astype(jnp.bfloat16))
            lower = silu_of_double(whole[BLOCK:, BLOCK:].astype(jnp.bfloat16))
            weights = jnp.concatenate(
                [
                    jnp.concatenate([upper, upper_near], axis=1),
                    jnp.concatenate([lower_edge - lower_near, lower], axis=1),
                ],
                axis=0,
            )
            total = dot32(weights, context[shared, value_of])
            heads_out[:BLOCK, of] = total[:BLOCK] + dot32(
                upper_edge - upper_near, context[oldest, value_of]
            )
            heads_out[BLOCK:, of] = total[BLOCK:] + dot32(lower_near, context[newest, value_of])
        gated = normalize(heads_out[...]) * gate[at].astype(jnp.float32)
        layer = dot32(gated.astype(jnp.bfloat16), w_out[...]) + events[at].astype(jnp.float32)
        position = piece * tokens + block * PAIR + lax.broadcasted_iota(jnp.int32, (PAIR, 1), 0)
        result[at] = jnp.where(position < live_ref[0], layer, 0.0).astype(result.dtype)

    def write(block):
        at = block_at(block)
        return pltpu.make_async_copy(result.at[at], out_ref.at[0, at], result_sems.at[block])

    @pl.loop(skipped, blocks)
    def _(block):
        attend(block)
        write(block).start()

    @pl.when(piece > 0)
    def _():
        halo.wait_recv()

    @pl.when(piece == 0)
    def _():
        context[:WINDOW] = jnp.zeros((WINDOW, 2 * width), context.dtype)

    @pl.loop(0, skipped)
    def _(block):
        attend(block)
        write(block).start()

    @pl.when(piece < pieces - 1)
    def _():
        halo.wait_send()

    @pl.loop(0, blocks)
    def _(block):
        write(block).wait()


def local(embed_table, lookup_ids, counts, event_order, hist_len, w_uvqk, w_out):
    shards = lax.axis_size("table")
    capacity = lookup_ids.shape[3]
    tokens = event_order.shape[2]
    rows, width = embed_table.shape
    part_rows = 1024 if rows % 1024 == 0 else rows
    slots = min(4, rows // part_rows)
    kind = jnp.bfloat16
    vmem = pl.BlockSpec(memory_space=pltpu.VMEM)
    smem = pl.BlockSpec(memory_space=pltpu.SMEM)
    anywhere = pl.BlockSpec(memory_space=pl.ANY)
    dma = pltpu.SemaphoreType.DMA
    return pl.pallas_call(
        layer_kernel,
        in_specs=[vmem, smem, vmem, smem, anywhere, anywhere, anywhere],
        out_specs=anywhere,
        out_shape=jax.ShapeDtypeStruct((1, tokens, width), kind),
        scratch_shapes=[
            pltpu.VMEM((shards, 1, capacity), jnp.int32),
            pltpu.SMEM((shards,), jnp.int32),
            pltpu.VMEM((shards, 1, capacity), jnp.int32),
            pltpu.SMEM((shards, 1, capacity), jnp.int32),
            pltpu.VMEM((slots, part_rows, width), kind),
            pltpu.VMEM((rows, width), jnp.float32),
            pltpu.VMEM((tokens, capacity), jnp.int32),
            pltpu.VMEM((capacity, width), jnp.float32),
            pltpu.VMEM((shards, capacity, width), kind),
            pltpu.VMEM((shards, capacity, width), kind),
            dma((slots,)),
            dma,
            dma((shards,)),
            dma((shards,)),
            dma((shards,)),
            dma((shards,)),
            pltpu.VMEM(w_uvqk.shape, kind),
            pltpu.VMEM(w_out.shape, kind),
            dma((2,)),
            pltpu.VMEM((tokens, width), kind),
            pltpu.VMEM((tokens, width), kind),
            pltpu.VMEM((tokens, width), kind),
            pltpu.VMEM((WINDOW + tokens, 2 * width), kind),
            pltpu.VMEM((PAIR, width), jnp.float32),
            pltpu.VMEM((tokens, width), kind),
            dma((tokens // PAIR,)),
            dma,
            dma,
        ],
        compiler_params=pltpu.CompilerParams(
            collective_id=0, has_side_effects=True, vmem_limit_bytes=VMEM_LIMIT
        ),
        cost_estimate=pl.CostEstimate(
            flops=2 * tokens * shards * capacity * width
            + 10 * tokens * width * width
            + 4 * tokens * (WINDOW + BLOCK) * width,
            bytes_accessed=2 * rows * width + 2 * tokens * width + 10 * width * width,
            transcendentals=4 * tokens * width + tokens * WINDOW * HEADS,
        ),
        name="layer",
    )(lookup_ids, counts, event_order, hist_len, embed_table, w_uvqk, w_out)


def solution(mesh):
    in_specs = (
        P("table", None),
        P("table", "seq", None, None),
        P("table", "seq", None),
        P("table", "seq", None),
        P("table"),
        P(),
        P(),
    )
    out_specs = P("table", "seq", None)
    return jax.shard_map(local, mesh=mesh, in_specs=in_specs, out_specs=out_specs, check_vma=False)
```

```python
import jax
import jax.numpy as jnp
from jax import lax
from jax.experimental import pallas as pl
from jax.experimental.pallas import tpu as pltpu
from jax.sharding import PartitionSpec as P

HEADS = 4
WINDOW = 1024
BLOCK = 256
PAIR = 2 * BLOCK
PLACED = 2048
LANES = 128
VMEM_LIMIT = 60 * 1024 * 1024


def normalize(values):
    average = jnp.mean(values, axis=-1, keepdims=True)
    centered = values - average
    spread = jnp.mean(centered * centered, axis=-1, keepdims=True)
    return centered * lax.rsqrt(spread + 1e-05)


def silu_of_double(half):
    return half + half * jnp.tanh(half)


def scores_of(queries, keys):
    return lax.dot_general(
        queries, keys, (((1,), (1,)), ((), ())), preferred_element_type=jnp.float32
    )


def dot32(left, right):
    return jnp.dot(left, right, preferred_element_type=jnp.float32)


def peer_offset(step, count):
    if count % 2:
        return step + 1
    turn = step // 2
    away = (turn + 1) // 2
    far = count // 2 + away * (1 - 2 * (turn % 2))
    near = lax.rem(count - 1 - turn // 2 + (turn % 2) * (turn + 1), count)
    return jnp.where(step % 2 == 0, far, near)


def layer_kernel(
    lookup_ref,
    counts_ref,
    order_ref,
    live_ref,
    table_ref,
    w_in_ref,
    w_out_ref,
    out_ref,
    ids_ref,
    starts,
    ids_held,
    ids_scalar,
    staged,
    table_wide,
    rank_wide,
    rows_wide,
    sent,
    received,
    stage_sems,
    scalar_sem,
    ids_send_sems,
    ids_recv_sems,
    send_sems,
    recv_sems,
    w_in,
    w_out,
    weight_sems,
    events,
    gate,
    queries,
    context,
    heads_out,
    result,
    result_sems,
    halo_send_sem,
    halo_recv_sem,
):
    shards, capacity, width = sent.shape
    tokens = events.shape[0]
    slots, part_rows = staged.shape[0], staged.shape[1]
    parts = table_ref.shape[0] // part_rows
    me = lax.axis_index("table")
    piece, pieces = lax.axis_index("seq"), lax.axis_size("seq")
    mesh_ids = pl.DeviceIdType.MESH

    def stage(part):
        return pltpu.make_async_copy(
            table_ref.at[pl.ds(pl.multiple_of(part * part_rows, part_rows), part_rows)],
            staged.at[part % slots],
            stage_sems.at[part % slots],
        )

    for part in range(slots):
        stage(part).start()
    load_in = pltpu.make_async_copy(w_in_ref, w_in, weight_sems.at[0])
    load_out = pltpu.make_async_copy(w_out_ref, w_out, weight_sems.at[1])
    load_in.start()
    load_out.start()

    for shard in range(shards):
        ids_ref[shard] = lookup_ref[0, 0, shard : shard + 1]

    barrier = pltpu.get_barrier_semaphore()

    @pl.loop(1, shards)
    def _(offset):
        peer = lax.rem(me + offset, shards)
        pl.semaphore_signal(barrier, inc=1, device_id={"table": peer}, device_id_type=mesh_ids)

    @pl.when(piece > 0)
    def _():
        pl.semaphore_signal(barrier, inc=1, device_id={"seq": piece - 1}, device_id_type=mesh_ids)

    @pl.when(piece < pieces - 1)
    def _():
        pl.semaphore_signal(barrier, inc=1, device_id={"seq": piece + 1}, device_id_type=mesh_ids)

    neighbours = jnp.where(piece > 0, 1, 0) + jnp.where(piece < pieces - 1, 1, 0)
    pl.semaphore_wait(barrier, shards - 1 + neighbours)

    def send_ids(offset):
        peer = lax.rem(me + offset, shards)
        return pltpu.make_async_remote_copy(
            src_ref=ids_ref.at[peer],
            dst_ref=ids_held.at[me],
            send_sem=ids_send_sems.at[offset],
            recv_sem=ids_recv_sems.at[me],
            device_id={"table": peer},
            device_id_type=mesh_ids,
        )

    def take_ids(source):
        return pltpu.make_async_remote_copy(
            src_ref=ids_ref.at[source],
            dst_ref=ids_held.at[source],
            send_sem=ids_send_sems.at[0],
            recv_sem=ids_recv_sems.at[source],
            device_id={"table": source},
            device_id_type=mesh_ids,
        )

    @pl.loop(1, shards)
    def _(offset):
        send_ids(offset).start()

    ids_held[me] = ids_ref[me]
    start = jnp.int32(0)
    for shard in range(shards):
        starts[shard] = start
        start = start + counts_ref[0, 0, shard]

    for first in range(0, tokens, LANES):
        ranks = order_ref[0, :, first : first + LANES]
        ranks = jnp.transpose(jnp.broadcast_to(ranks, (LANES, LANES)))
        for column in range(0, capacity, LANES):
            count = min(LANES, capacity - column)
            rank_wide[first : first + LANES, column : column + count] = ranks[:, :count]

    for part in range(parts):
        stage(part).wait()

        @pl.loop(0, part_rows, step=64)
        def _(first):
            first = pl.multiple_of(first, 64)
            target = pl.multiple_of(part * part_rows + first, 64)
            table_wide[pl.ds(target, 64)] = staged[part % slots, pl.ds(first, 64)].astype(
                jnp.float32
            )

        if part + slots < parts:
            stage(part + slots).start()

    @pl.loop(1, shards)
    def _(offset):
        take_ids(lax.rem(me + offset, shards)).wait_recv()

    to_scalar = pltpu.make_async_copy(ids_held, ids_scalar, scalar_sem)
    to_scalar.start()
    to_scalar.wait()

    def gather(peer):
        @pl.loop(0, capacity, step=16)
        def _(first):
            for i in range(16):
                row = ids_scalar[peer, 0, first + i]
                rows_wide[pl.ds(first + i, 1)] = table_wide[pl.ds(row, 1)]

        return rows_wide[...].astype(jnp.bfloat16)

    def send_rows(offset):
        peer = lax.rem(me + offset, shards)
        return pltpu.make_async_remote_copy(
            src_ref=sent.at[offset],
            dst_ref=received.at[me],
            send_sem=send_sems.at[offset],
            recv_sem=recv_sems.at[me],
            device_id={"table": peer},
            device_id_type=mesh_ids,
        )

    def take_rows(source):
        return pltpu.make_async_remote_copy(
            src_ref=sent.at[0],
            dst_ref=received.at[source],
            send_sem=send_sems.at[0],
            recv_sem=recv_sems.at[source],
            device_id={"table": source},
            device_id_type=mesh_ids,
        )

    @pl.loop(0, shards - 1)
    def _(step):
        offset = peer_offset(step, shards)
        sent[offset] = gather(lax.rem(me + offset, shards))
        send_rows(offset).start()

    received[me] = gather(me)

    def place(source, add):
        slot = lax.broadcasted_iota(jnp.int32, (1, capacity), 1)
        keys = jnp.where(slot < counts_ref[0, 0, source], starts[source] + slot, -1)

        for first in range(0, tokens, PLACED):
            at = slice(first, first + PLACED)
            chosen = jnp.where(rank_wide[at] == keys, 1.0, 0.0).astype(jnp.bfloat16)
            found = jnp.dot(chosen, received[source], preferred_element_type=jnp.float32)
            found = found.astype(jnp.bfloat16)
            events[at] = events[at] + found if add else found

    place(me, False)

    @pl.loop(0, shards - 1)
    def _(step):
        source = lax.rem(me + shards - peer_offset(step, shards), shards)
        take_rows(source).wait_recv()
        place(source, True)

    @pl.loop(1, shards)
    def _(offset):
        send_ids(offset).wait_send()
        send_rows(offset).wait_send()

    load_in.wait()
    load_out.wait()
    query_scale = 0.5 * (width // HEADS) ** (-0.5)
    blocks = tokens // PAIR
    skipped = WINDOW // PAIR

    def block_at(block, offset=0, count=PAIR):
        first = block * PAIR + offset
        return pl.ds(first if isinstance(first, int) else pl.multiple_of(first, BLOCK), count)

    def project(block):
        at = block_at(block)
        normed = (0.5 * normalize(events[at].astype(jnp.float32))).astype(jnp.bfloat16)

        def columns(first, kind):
            return silu_of_double(dot32(normed, w_in[:, first : first + width]).astype(kind))

        gate[at] = columns(0, jnp.float32).astype(gate.dtype)
        queries[at] = (columns(width, jnp.bfloat16).astype(jnp.float32) * query_scale).astype(queries.dtype)
        own = block_at(block, WINDOW)
        context[own, :width] = columns(2 * width, context.dtype)
        context[own, width:] = columns(3 * width, context.dtype)

    for block in range(blocks - skipped, blocks):
        project(block)

    halo = pltpu.make_async_remote_copy(
        src_ref=context.at[pl.ds(tokens, WINDOW)],
        dst_ref=context.at[pl.ds(0, WINDOW)],
        send_sem=halo_send_sem,
        recv_sem=halo_recv_sem,
        device_id={"seq": lax.rem(piece + 1, pieces)},
        device_id_type=mesh_ids,
    )

    @pl.when(piece < pieces - 1)
    def _():
        halo.start()

    for block in range(blocks - skipped):
        project(block)

    row = lax.broadcasted_iota(jnp.int32, (BLOCK, BLOCK), 0)
    column = lax.broadcasted_iota(jnp.int32, (BLOCK, BLOCK), 1)
    near = column <= row
    near_weight = near.astype(jnp.float32).astype(jnp.bfloat16)
    head_width = width // HEADS

    def attend(block, held, between):
        at = block_at(block)
        oldest = block_at(block, 0, BLOCK)
        newest = block_at(block, WINDOW + BLOCK, BLOCK)
        shared = block_at(block, BLOCK, WINDOW)
        for head in range(HEADS):
            if head == 1:
                between()
            of = slice(head * head_width, (head + 1) * head_width)
            value_of = slice(width + head * head_width, width + (head + 1) * head_width)
            asked = queries[at, of]
            whole = scores_of(asked, context[shared, of])
            upper_far = scores_of(asked[:BLOCK], context[oldest, of])
            lower_near = scores_of(asked[BLOCK:], context[newest, of])
            upper_edge = jnp.where(near, whole[:BLOCK, WINDOW - BLOCK :], upper_far)
            lower_edge = jnp.where(near, lower_near, whole[BLOCK:, :BLOCK])
            upper_edge = silu_of_double(upper_edge.astype(jnp.bfloat16))
            lower_edge = silu_of_double(lower_edge.astype(jnp.bfloat16))
            upper_near = upper_edge * near_weight
            lower_near = lower_edge * near_weight
            upper = silu_of_double(whole[:BLOCK, : WINDOW - BLOCK].astype(jnp.bfloat16))
            lower = silu_of_double(whole[BLOCK:, BLOCK:].astype(jnp.bfloat16))
            weights = jnp.concatenate(
                [
                    jnp.concatenate([upper, upper_near], axis=1),
                    jnp.concatenate([lower_edge - lower_near, lower], axis=1),
                ],
                axis=0,
            )
            total = dot32(weights, context[shared, value_of])
            heads_out[held, :BLOCK, of] = total[:BLOCK] + dot32(
                upper_edge - upper_near, context[oldest, value_of]
            )
            heads_out[held, BLOCK:, of] = total[BLOCK:] + dot32(lower_near, context[newest, value_of])

    def finish(block, held):
        at = block_at(block)
        gated = normalize(heads_out[held]) * gate[at].astype(jnp.float32)
        layer = dot32(gated.astype(jnp.bfloat16), w_out[...]) + events[at].astype(jnp.float32)
        position = piece * tokens + block * PAIR + lax.broadcasted_iota(jnp.int32, (PAIR, 1), 0)
        result[at] = jnp.where(position < live_ref[0], layer, 0.0).astype(result.dtype)

    def write(block):
        at = block_at(block)
        return pltpu.make_async_copy(result.at[at], out_ref.at[0, at], result_sems.at[block])

    def write_finished(block, held):
        finish(block, held)
        write(block).start()

    order = [*range(skipped, blocks), *range(skipped)]

    def attend_turns(first, last):
        for turn in range(first, last):
            between = lambda: None
            if turn > 0:
                between = lambda: write_finished(order[turn - 1], (turn - 1) % 2)
            attend(order[turn], turn % 2, between)

    attend_turns(0, blocks - skipped)

    @pl.when(piece > 0)
    def _():
        halo.wait_recv()

    @pl.when(piece == 0)
    def _():
        context[:WINDOW] = jnp.zeros((WINDOW, 2 * width), context.dtype)

    attend_turns(blocks - skipped, blocks)
    write_finished(order[-1], (blocks - 1) % 2)

    @pl.when(piece < pieces - 1)
    def _():
        halo.wait_send()

    @pl.loop(0, blocks)
    def _(block):
        write(block).wait()


def local(embed_table, lookup_ids, counts, event_order, hist_len, w_uvqk, w_out):
    shards = lax.axis_size("table")
    capacity = lookup_ids.shape[3]
    tokens = event_order.shape[2]
    rows, width = embed_table.shape
    part_rows = 1024 if rows % 1024 == 0 else rows
    slots = min(4, rows // part_rows)
    kind = jnp.bfloat16
    vmem = pl.BlockSpec(memory_space=pltpu.VMEM)
    smem = pl.BlockSpec(memory_space=pltpu.SMEM)
    anywhere = pl.BlockSpec(memory_space=pl.ANY)
    dma = pltpu.SemaphoreType.DMA
    return pl.pallas_call(
        layer_kernel,
        in_specs=[vmem, smem, vmem, smem, anywhere, anywhere, anywhere],
        out_specs=anywhere,
        out_shape=jax.ShapeDtypeStruct((1, tokens, width), kind),
        scratch_shapes=[
            pltpu.VMEM((shards, 1, capacity), jnp.int32),
            pltpu.SMEM((shards,), jnp.int32),
            pltpu.VMEM((shards, 1, capacity), jnp.int32),
            pltpu.SMEM((shards, 1, capacity), jnp.int32),
            pltpu.VMEM((slots, part_rows, width), kind),
            pltpu.VMEM((rows, width), jnp.float32),
            pltpu.VMEM((tokens, capacity), jnp.int32),
            pltpu.VMEM((capacity, width), jnp.float32),
            pltpu.VMEM((shards, capacity, width), kind),
            pltpu.VMEM((shards, capacity, width), kind),
            dma((slots,)),
            dma,
            dma((shards,)),
            dma((shards,)),
            dma((shards,)),
            dma((shards,)),
            pltpu.VMEM(w_uvqk.shape, kind),
            pltpu.VMEM(w_out.shape, kind),
            dma((2,)),
            pltpu.VMEM((tokens, width), kind),
            pltpu.VMEM((tokens, width), kind),
            pltpu.VMEM((tokens, width), kind),
            pltpu.VMEM((WINDOW + tokens, 2 * width), kind),
            pltpu.VMEM((2, PAIR, width), jnp.float32),
            pltpu.VMEM((tokens, width), kind),
            dma((tokens // PAIR,)),
            dma,
            dma,
        ],
        compiler_params=pltpu.CompilerParams(
            collective_id=0, has_side_effects=True, vmem_limit_bytes=VMEM_LIMIT
        ),
        cost_estimate=pl.CostEstimate(
            flops=2 * tokens * shards * capacity * width
            + 10 * tokens * width * width
            + 4 * tokens * (WINDOW + BLOCK) * width,
            bytes_accessed=2 * rows * width + 2 * tokens * width + 10 * width * width,
            transcendentals=4 * tokens * width + tokens * WINDOW * HEADS,
        ),
        name="layer",
    )(lookup_ids, counts, event_order, hist_len, embed_table, w_uvqk, w_out)


def solution(mesh):
    in_specs = (
        P("table", None),
        P("table", "seq", None, None),
        P("table", "seq", None),
        P("table", "seq", None),
        P("table"),
        P(),
        P(),
    )
    out_specs = P("table", "seq", None)
    return jax.shard_map(local, mesh=mesh, in_specs=in_specs, out_specs=out_specs, check_vma=False)
```
